32 devices in a mesh: gx: 16 (over z, y, core), gy: 2 (over x).
Axes of the slice: x: 2, y: 2, z: 4, core: 2. Of those that a mesh axis runs over, the one named last changes fastest.
Arguments:
- rhs: float32 [8, 32, 16, 128], P(None, 'gx', 'gy'), may hold values from -6 to 6
- classes: int32 [32, 16, 128], P('gx', 'gy'), may hold values from 0 to 3
- supports: int32 [32, 16, 128], P('gx', 'gy'), may hold values 0 or 1
Outputs:
- solution: float32 [8, 32, 16, 128], P(None, 'gx', 'gy')
- residual: float32 [8, 32, 16, 128], P(None, 'gx', 'gy')
- new_direction: float32 [8, 32, 16, 128], P(None, 'gx', 'gy')
The draws below stay inside these ranges and needn't reach their ends.
Inputs may be any that keep to these rules, and one draw needn't show every extreme that they name: `supports`: 1 marks a grounded node.
All inputs are finite; a program needn't handle non-finite values. No bound on the sum of `supports` on one device may be relied on, other than what follows from the above.
Results may differ from the reference program's by a relative error of at most 0.0003.
Values sent between devices are 32-bit elements; how exact they have to be, the bound alone decides.
A program may use at most 64 MiB of HBM per device.

```python
import jax
import jax.numpy as jnp
from jax import lax

RHS = 8
COARSE_SWEEPS = 2
NX = 32
NY = 16
NZ = 128


def with_ends(values, own_key, least, top_value):
    dims = values.shape
    spot = [jax.random.randint(jax.random.fold_in(own_key, axis), (), 0, dims[axis]) for axis in range(len(dims))]
    values = values.at[tuple(spot)].set(least)
    longest = dims.index(max(dims))
    spot[longest] = (spot[longest] + 1) % dims[longest]
    return values.at[tuple(spot)].set(top_value)


def block_levels(rng, dims, split, least, largest):
    def one(dim, shards_of):
        heights = jax.random.uniform(jax.random.fold_in(jax.random.fold_in(rng, 6), dim), (shards_of,), jnp.float32, least / len(split), largest / len(split))
        return jnp.repeat(jnp.exp(heights), dims[dim] // shards_of).reshape((-1,) + (1,) * (len(dims) - dim - 1))

    loudness = one(*split[0])
    for cut in split[1:]:
        loudness = loudness * one(*cut)
    return loudness


def scatter_about(own_key, dims, deviation, most, cuts=(), dtype=jnp.bfloat16):
    gain = block_levels(own_key, dims, cuts, -0.22, 0.18) if cuts else 1.0
    array = jax.random.normal(own_key, dims, jnp.float32) * deviation * gain
    return jnp.minimum(jnp.maximum(array, -most), most).astype(dtype)


def setup_inputs(seed: int = 0) -> dict:
    splits = jax.random.split(jax.random.key(seed), 4)
    return {
        "rhs": scatter_about(splits[0], (RHS, NX, NY, NZ), 1.0, 6.0, ((1, 16), (2, 2)), jnp.float32),
        "classes": with_ends(jax.random.randint(splits[1], (NX, NY, NZ), 0, 4), jax.random.fold_in(splits[1], 1), 0, 3).astype(jnp.int32),
        "supports": with_ends((jax.random.randint(splits[2], (NX, NY, NZ), 0, 8) < 1).astype(jnp.int32), jax.random.fold_in(splits[2], 1), 0, 1),
    }


SPRING = 8.0
OMEGA = 0.6
DAMP = 0.5
SELF_WEIGHT = 5.0 / 12.0

def stiffness(classes):
    density = (classes.astype(jnp.float32) + 1.0) / 4.0
    return 0.001 + density * density * density

def hex_product(padded, scale_ext):
    nx = scale_ext.shape[0] - 1
    ny = scale_ext.shape[1] - 1
    nz = scale_ext.shape[2] - 1
    corners = {}
    for a in (0, 1):
        for b in (0, 1):
            for c in (0, 1):
                corners[a, b, c] = padded[..., a:a + nx + 1, b:b + ny + 1, c:c + nz + 1]
    summed = sum(corners.values())
    result = None
    for key in corners:
        a, b, c = key
        corner = corners[key]
        adjacent = corners[1 - a, b, c] + corners[a, 1 - b, c] + corners[a, b, 1 - c]
        weighted = scale_ext * (SELF_WEIGHT * corner + adjacent / 12.0 - summed / 12.0)
        piece = weighted[..., 1 - a:1 - a + nx, 1 - b:1 - b + ny, 1 - c:1 - c + nz]
        result = piece if result is None else result + piece
    return result

def prolong(field):
    k, a, b, c = field.shape
    wide = jnp.broadcast_to(field[:, :, None, :, None, :, None], (k, a, 2, b, 2, c, 2))
    return wide.reshape(k, 2 * a, 2 * b, 2 * c)

def restrict(field):
    k, a, b, c = field.shape
    return field.reshape(k, a // 2, 2, b // 2, 2, c // 2, 2).sum(axis=(2, 4, 6))

def inner_block(left, right):
    count = left.shape[0]
    return jnp.dot(left.reshape(count, -1), right.reshape(count, -1).T, precision=lax.Precision.HIGHEST)

def recombine(coef, field):
    count = field.shape[0]
    return jnp.dot(coef.T, field.reshape(count, -1), precision=lax.Precision.HIGHEST).reshape(field.shape)

def spd_solve(matrix, right):
    lower = jnp.linalg.cholesky(matrix)
    middle = lax.linalg.triangular_solve(lower, right, left_side=True, lower=True)
    return lax.linalg.triangular_solve(lower, middle, left_side=True, lower=True, transpose_a=True)

def reference(rhs, classes, supports):
    scale_ext = jnp.pad(stiffness(classes), ((0, 1), (0, 1), (0, 1)))
    support = supports.astype(jnp.float32)
    nx, ny, nz = support.shape
    diagonal = SPRING * support
    for a in (0, 1):
        for b in (0, 1):
            for c in (0, 1):
                diagonal = diagonal + scale_ext[a:a + nx, b:b + ny, c:c + nz] / 3.0
    coarse_step = DAMP / restrict(diagonal[None])[0]

    def apply_one(field):
        padded = jnp.pad(field, ((1, 1), (1, 1), (1, 1)))
        return hex_product(padded, scale_ext) + SPRING * support * field

    def fine_apply(field):
        return lax.map(apply_one, field)

    def precondition(source):
        smoothed = OMEGA * source / diagonal
        coarse_res = restrict(source - fine_apply(smoothed))
        coarse = coarse_step * coarse_res
        for sweep in range(COARSE_SWEEPS):
            coarse = coarse + coarse_step * (coarse_res - restrict(fine_apply(prolong(coarse))))
        smoothed = smoothed + prolong(coarse)
        return smoothed + OMEGA * (source - fine_apply(smoothed)) / diagonal
    first_prec = precondition(rhs)
    applied = fine_apply(first_prec)
    curvature = inner_block(first_prec, applied)
    curvature = 0.5 * (curvature + curvature.T)
    projection = inner_block(first_prec, rhs)
    step_coef = spd_solve(curvature, projection)
    solution = recombine(step_coef, first_prec)
    residual = rhs - recombine(step_coef, applied)
    next_prec = precondition(residual)
    coupling = inner_block(applied, next_prec)
    turn_coef = -spd_solve(curvature, coupling)
    new_direction = next_prec + recombine(turn_coef, first_prec)
    return (solution, residual, new_direction)
```

```python
import functools

import jax
import jax.numpy as jnp
from jax import lax
from jax.experimental import pallas as pl
from jax.experimental.pallas import tpu as pltpu
from jax.sharding import PartitionSpec as P

SPRING = 8.0
OMEGA = 0.6
DAMP = 0.5
HALO = 2

MESH = pl.DeviceIdType.MESH
EXACT = lax.Precision.HIGHEST


def axis_ids(shape, dim):
    return lax.broadcasted_iota(jnp.int32, shape, dim)


def before(u, dim):
    return jnp.where(axis_ids(u.shape, dim) == 0, 0.0, pltpu.roll(u, 1, dim))


def after(u, dim):
    size = u.shape[dim]
    return jnp.where(axis_ids(u.shape, dim) == size - 1, 0.0, pltpu.roll(u, size - 1, dim))


def pair_sum(u, dim):
    size = u.shape[dim]
    even = axis_ids(u.shape, dim) % 2 == 0
    return u + jnp.where(even, pltpu.roll(u, size - 1, dim), pltpu.roll(u, 1, dim))


def block_sum(u):
    planes, rows, lanes = u.shape
    pairs = u.reshape(planes // 2, 2, rows, lanes)
    return pair_sum(pair_sum(pairs[:, 0] + pairs[:, 1], 1), 2)


def spread(c):
    cells, rows, lanes = c.shape
    return jnp.broadcast_to(c[:, None], (cells, 2, rows, lanes)).reshape(2 * cells, rows, lanes)


def hex_apply(u, e1, e2, e3):
    back = before(u, 2)
    s, d = u + back, u - back
    sb, db = before(s, 1), before(d, 1)
    ss, ds, sd, dd = s + sb, s - sb, d + db, d - db
    m00 = e1 * (ss[1:] - ss[:-1])
    s10, d10 = e1 * (ds[1:] + ds[:-1]), e2 * (ds[1:] - ds[:-1])
    s01, d01 = e1 * (sd[1:] + sd[:-1]), e2 * (sd[1:] - sd[:-1])
    s11, d11 = e2 * (dd[1:] + dd[:-1]), e3 * (dd[1:] - dd[:-1])
    t00 = m00[:-1] - m00[1:]
    t10 = (s10 + d10)[:-1] + (s10 - d10)[1:]
    t01 = (s01 + d01)[:-1] + (s01 - d01)[1:]
    t11 = (s11 + d11)[:-1] + (s11 - d11)[1:]
    ts = (t00 + t10) + after(t00 - t10, 1)
    td = (t01 + t11) + after(t01 - t11, 1)
    return (ts + td) + after(ts - td, 2)


def kernel(
    ngx, ngy,
    rhs_ref, classes_ref, supports_ref, sol_ref, res_ref, dir_ref,
    mine, cext, rext, scales, weight, spring, cstep,
    own_c, halo_c, halo_a, fields, returned, part, first_sums, group_sum, last_sums,
    gc_send, gc_recv, gr_send, gr_recv, x_send, x_recv, b_send, b_recv, a_send, a_recv, q_send, q_recv,
):
    count, lx, ly, nz = rhs_ref.shape
    group = count // ngy
    groups = ngx // group
    slots = group + 2 * HALO
    rows = ngy * ly
    planes = 2 * slots
    gx, gy = lax.axis_index("gx"), lax.axis_index("gy")
    g, s = gx // group, gx % group
    me = s * ngy + gy

    def member(at_group, j):
        return (at_group * group + j // ngy, j % ngy)

    def exists(at_group):
        return jnp.logical_and(at_group >= 0, at_group < groups)

    def guarded(condition, action):
        pl.when(condition)(action)

    barrier = pltpu.get_barrier_semaphore()

    def greet(target):
        pl.semaphore_signal(barrier, inc=1, device_id=target, device_id_type=MESH)

    for j in range(count):
        for dg in (-1, 0, 1):
            ok = exists(g + dg) if dg else j != me
            guarded(ok, functools.partial(greet, member(g + dg, j)))
    for q in range(groups):
        guarded(jnp.abs(q - g) > 1, functools.partial(greet, (q * group + s, gy)))
    below, above = (g > 0).astype(jnp.int32), (g < groups - 1).astype(jnp.int32)
    expected = (count - 1) + count * (below + above) + (groups - 1 - below - above)

    density = (classes_ref[...].astype(jnp.float32) + 1.0) / 4.0
    mine[0] = 0.001 + density * density * density
    mine[1] = supports_ref[...].astype(jnp.float32)

    def clear_below():
        cext[:, 0:HALO] = jnp.zeros((2, HALO, 2, ngy, ly, nz), jnp.float32)
        rext[0:HALO] = jnp.zeros((HALO, 2, ngy, ly, nz), jnp.float32)
        for call in range(2):
            halo_c[call, 0] = jnp.zeros((HALO, rows, nz), jnp.float32)
        halo_a[0] = jnp.zeros((2, 2, ngy, ly, nz), jnp.float32)

    def clear_above():
        cext[:, slots - HALO :] = jnp.zeros((2, HALO, 2, ngy, ly, nz), jnp.float32)
        rext[slots - HALO :] = jnp.zeros((HALO, 2, ngy, ly, nz), jnp.float32)
        for call in range(2):
            halo_c[call, 1] = jnp.zeros((HALO, rows, nz), jnp.float32)
        halo_a[1] = jnp.zeros((2, 2, ngy, ly, nz), jnp.float32)

    guarded(g == 0, clear_below)
    guarded(g == groups - 1, clear_above)
    pl.semaphore_wait(barrier, expected)

    def coef_copy(dg, j):
        slot = s + HALO - dg * group
        return pltpu.make_async_remote_copy(
            src_ref=mine, dst_ref=cext.at[:, slot, :, gy],
            send_sem=gc_send.at[dg + 1, j], recv_sem=gc_recv.at[slot, gy],
            device_id=member(g + dg, j), device_id_type=MESH)

    def rhs_copy(dg, j):
        slot = s + HALO - dg * group
        return pltpu.make_async_remote_copy(
            src_ref=rhs_ref.at[j], dst_ref=rext.at[slot, :, gy],
            send_sem=gr_send.at[dg + 1, j], recv_sem=gr_recv.at[slot, gy],
            device_id=member(g + dg, j), device_id_type=MESH)

    def sends(dg, j):
        if dg == 0:
            return j != me
        slot = s + HALO - dg * group
        return exists(g + dg) & (slot >= 0) & (slot < slots)

    for make in (coef_copy, rhs_copy):
        for dg in (-1, 1, 0):
            for j in range(count):
                guarded(sends(dg, j), lambda: make(dg, j).start())
    cext[:, s + HALO, :, gy] = mine[...]
    rext[s + HALO, :, gy] = rhs_ref[me]

    def arrives(slot, y):
        from_group = g + (slot - HALO) // group
        if HALO <= slot < HALO + group:
            return (slot - HALO) * ngy + y != me
        return exists(from_group)

    def wait_coef(slot, y):
        pltpu.make_async_remote_copy(
            src_ref=mine, dst_ref=cext.at[:, slot, :, y], send_sem=gc_send.at[0, 0],
            recv_sem=gc_recv.at[slot, y], device_id=(gx, gy), device_id_type=MESH).wait_recv()

    def wait_rhs(slot, y):
        pltpu.make_async_remote_copy(
            src_ref=rhs_ref.at[0], dst_ref=rext.at[slot, :, y], send_sem=gr_send.at[0, 0],
            recv_sem=gr_recv.at[slot, y], device_id=(gx, gy), device_id_type=MESH).wait_recv()

    for slot in range(slots):
        for y in range(ngy):
            guarded(arrives(slot, y), functools.partial(wait_coef, slot, y))

    lo, hi = 2 * HALO, planes - 2 * HALO
    plane = axis_ids((planes, rows, nz), 0) + (2 * group * g - 2 * HALO)
    inside = (plane >= 0) & (plane < ngx * lx)
    e = jnp.where(inside, cext[0].reshape(planes, rows, nz), 0.0)
    scales[0] = e * (1.0 / 16.0)
    scales[1] = e * (1.0 / 24.0)
    scales[2] = e * (1.0 / 48.0)
    spring[...] = SPRING * cext[1].reshape(planes, rows, nz)
    around = e[:-1] + e[1:]
    around = around + after(around, 1)
    around = around + after(around, 2)
    diagonal = around * (1.0 / 3.0) + spring[0 : planes - 1]
    real = inside[:-1]
    weight[0 : planes - 1] = jnp.where(real, OMEGA / jnp.where(real, diagonal, 1.0), 0.0)
    sums = block_sum(jnp.where(real, diagonal, 0.0)[lo - 2 : hi + 2])
    cstep[...] = jnp.where(sums > 0.0, DAMP / jnp.where(sums > 0.0, sums, 1.0), 0.0)

    def apply(u, start, stop):
        product = hex_apply(u, scales[0, start : stop + 1], scales[1, start : stop + 1], scales[2, start : stop + 1])
        return product + spring[start:stop] * u[1:-1]

    def swap_edges(low_src, high_src, low_dst, high_dst, k):
        down = pltpu.make_async_remote_copy(
            src_ref=low_src, dst_ref=high_dst, send_sem=x_send.at[k, 0], recv_sem=x_recv.at[k, 1],
            device_id=(jnp.maximum(gx - group, 0), gy), device_id_type=MESH)
        up = pltpu.make_async_remote_copy(
            src_ref=high_src, dst_ref=low_dst, send_sem=x_send.at[k, 1], recv_sem=x_recv.at[k, 0],
            device_id=(jnp.minimum(gx + group, ngx - 1), gy), device_id_type=MESH)
        guarded(g > 0, down.start)
        guarded(g < groups - 1, up.start)
        return down, up

    def finish_edges(down, up):
        guarded(g > 0, up.wait_recv)
        guarded(g < groups - 1, down.wait_recv)

    def drain_edges(down, up):
        guarded(g > 0, down.wait_send)
        guarded(g < groups - 1, up.wait_send)

    pending = []

    def corrected(source, call):
        z = source * weight[lo - 3 : hi + 3]
        rest = block_sum(source[1:-1] - apply(z, lo - 2, hi + 2))
        c = cstep[...] * rest
        fixed = block_sum(apply(spread(c)[1:-1], lo, hi))
        own_c[call] = c[1:-1] + cstep[1 : group + 1] * (rest[1:-1] - fixed)
        copies = swap_edges(
            own_c.at[call, pl.ds(0, HALO)], own_c.at[call, pl.ds(group - HALO, HALO)],
            halo_c.at[call, 0], halo_c.at[call, 1], call)
        pending.append(copies)
        finish_edges(*copies)
        c = jnp.concatenate([halo_c[call, 0], own_c[call], halo_c[call, 1]], axis=0)
        c = c[1:-1] + cstep[...] * (rest - block_sum(apply(spread(c)[1:-1], lo - 2, hi + 2)))
        return z[1:-1] + spread(c)

    for slot in range(slots):
        for y in range(ngy):
            guarded(arrives(slot, y), functools.partial(wait_rhs, slot, y))
    source = rext[...].reshape(planes, rows, nz)[lo - 3 : hi + 3]
    z = corrected(source, 0)
    first = z[1:-1] + weight[lo - 1 : hi + 1] * (source[2:-2] - apply(z, lo - 1, hi + 1))
    applied = apply(first, lo, hi)

    def shaped(u):
        return u.reshape(group, 2, ngy, ly, nz)

    fields[0] = shaped(first[1:-1])
    fields[1] = shaped(applied)
    own_a = fields.at[1]
    halo_src_low = own_a.at[pl.ds(0, 2)]
    halo_src_high = own_a.at[pl.ds(group - 2, 2)]
    copies = swap_edges(halo_src_low, halo_src_high, halo_a.at[0], halo_a.at[1], 2)
    pending.append(copies)

    def back_copy(k, f, n, j):
        return pltpu.make_async_remote_copy(
            src_ref=fields.at[pl.ds(f, n), j // ngy, :, j % ngy], dst_ref=returned.at[pl.ds(f, n), me],
            send_sem=b_send.at[k, j], recv_sem=b_recv.at[k, me],
            device_id=member(g, j), device_id_type=MESH)

    def wait_back(k, f, n, j):
        pltpu.make_async_remote_copy(
            src_ref=fields.at[pl.ds(f, n), 0, :, 0], dst_ref=returned.at[pl.ds(f, n), j],
            send_sem=b_send.at[k, j], recv_sem=b_recv.at[k, j],
            device_id=(gx, gy), device_id_type=MESH).wait_recv()

    def send_back(k, f, n):
        for j in range(count):
            guarded(j != me, lambda: back_copy(k, f, n, j).start())
        for i in range(f, f + n):
            returned[i, me] = fields[i, s, :, gy]

    send_back(0, 0, 2)
    finish_edges(*copies)
    low = halo_a[0].reshape(4, rows, nz)[1:]
    high = halo_a[1].reshape(4, rows, nz)[:-1]
    source = jnp.concatenate([low, applied, high], axis=0)
    z = corrected(source, 1)[1:-1]
    own = slice(lo, hi)
    fields[2] = shaped(z[1:-1] + weight[own] * (applied - apply(z, lo, hi)))
    send_back(1, 2, 1)
    for k, f, n in ((0, 0, 2), (1, 2, 1)):
        for j in range(count):
            guarded(j != me, functools.partial(wait_back, k, f, n, j))

    def flat(block):
        parts = []
        for a in range(lx):
            turned = jnp.swapaxes(block[:, a], 0, 1)
            parts += [turned[b] for b in range(ly)]
        return jnp.concatenate(parts, axis=1)

    field, product, twice = flat(returned[0]), flat(returned[1]), flat(returned[2])
    given = flat(rhs_ref[...])
    none = jnp.zeros_like(field)
    left = jnp.concatenate([field, product], axis=1)
    right = jnp.concatenate([
        jnp.concatenate([product, field], axis=1),
        jnp.concatenate([given, none], axis=1),
        jnp.concatenate([none, field], axis=1),
        jnp.concatenate([none, twice], axis=1),
        jnp.zeros((128 - 4 * count, 2 * field.shape[1]), jnp.float32)], axis=0)
    part[...] = lax.dot_general(
        left, right, (((1,), (1,)), ((), ())), precision=EXACT, preferred_element_type=jnp.float32)

    def sum_copy(j):
        return pltpu.make_async_remote_copy(
            src_ref=part, dst_ref=first_sums.at[me], send_sem=a_send.at[j], recv_sem=a_recv.at[me],
            device_id=member(g, j), device_id_type=MESH)

    def sum_wait(j):
        pltpu.make_async_remote_copy(
            src_ref=part, dst_ref=first_sums.at[j], send_sem=a_send.at[j], recv_sem=a_recv.at[j],
            device_id=(gx, gy), device_id_type=MESH).wait_recv()

    for j in range(count):
        guarded(j != me, lambda: sum_copy(j).start())
    first_sums[me] = part[...]
    for j in range(count):
        guarded(j != me, functools.partial(sum_wait, j))
    group_sum[...] = jnp.sum(first_sums[...], axis=0)

    def total_copy(q):
        return pltpu.make_async_remote_copy(
            src_ref=group_sum, dst_ref=last_sums.at[g], send_sem=q_send.at[q], recv_sem=q_recv.at[g],
            device_id=(q * group + s, gy), device_id_type=MESH)

    def total_wait(q):
        pltpu.make_async_remote_copy(
            src_ref=group_sum, dst_ref=last_sums.at[q], send_sem=q_send.at[q], recv_sem=q_recv.at[q],
            device_id=(gx, gy), device_id_type=MESH).wait_recv()

    for q in range(groups):
        guarded(q != g, lambda: total_copy(q).start())
    last_sums[g] = group_sum[...]
    for q in range(groups):
        guarded(q != g, functools.partial(total_wait, q))
    system = jnp.sum(last_sums[...], axis=0)

    lane = axis_ids(system.shape, 1)
    row = axis_ids(system.shape, 0)
    system = jnp.where(lane < count, 0.5 * system, system)
    for k in range(count):
        column = jnp.sum(jnp.where(lane == k, system, 0.0), axis=1, keepdims=True)
        pivot_row = system[k : k + 1]
        scaled = pivot_row / pivot_row[:, k : k + 1]
        system = jnp.where(row == k, scaled, system - column * scaled)

    def columns(n):
        return system[:, n * count : (n + 1) * count]

    step = columns(1)
    turn = jnp.dot(columns(3), step, precision=EXACT, preferred_element_type=jnp.float32) - columns(2)

    def mixed(coef, u):
        return lax.dot_general(
            coef, u, (((0,), (0,)), ((), ())), precision=EXACT, preferred_element_type=jnp.float32)

    def put(ref, u):
        for a in range(lx):
            at = a * ly
            block = jnp.stack([u[:, (at + b) * nz : (at + b + 1) * nz] for b in range(ly)], axis=0)
            ref[:, a] = jnp.swapaxes(block, 0, 1)

    put(sol_ref, mixed(step, field))
    put(res_ref, given - mixed(step, product))
    put(dir_ref, field + mixed(turn, field) - mixed(step, twice))

    for make in (coef_copy, rhs_copy):
        for dg in (-1, 1, 0):
            for j in range(count):
                guarded(sends(dg, j), lambda: make(dg, j).wait_send())
    for copies in pending:
        drain_edges(*copies)
    for k, f, n in ((0, 0, 2), (1, 2, 1)):
        for j in range(count):
            guarded(j != me, lambda: back_copy(k, f, n, j).wait_send())
    for j in range(count):
        guarded(j != me, lambda: sum_copy(j).wait_send())
    for q in range(groups):
        guarded(q != g, lambda: total_copy(q).wait_send())


def local(ngx, ngy, rhs, classes, supports):
    count, lx, ly, nz = rhs.shape
    group = count // ngy
    groups = ngx // group
    slots = group + 2 * HALO
    rows = ngy * ly
    planes = 2 * slots
    f32 = jnp.float32
    dma = pltpu.SemaphoreType.DMA
    return pl.pallas_call(
        functools.partial(kernel, ngx, ngy),
        out_shape=[jax.ShapeDtypeStruct(rhs.shape, f32)] * 3,
        in_specs=[pl.BlockSpec(memory_space=pltpu.VMEM)] * 3,
        out_specs=[pl.BlockSpec(memory_space=pltpu.VMEM)] * 3,
        scratch_shapes=[
            pltpu.VMEM((2, lx, ly, nz), f32),
            pltpu.VMEM((2, slots, 2, ngy, ly, nz), f32),
            pltpu.VMEM((slots, 2, ngy, ly, nz), f32),
            pltpu.VMEM((3, planes, rows, nz), f32),
            pltpu.VMEM((planes, rows, nz), f32),
            pltpu.VMEM((planes, rows, nz), f32),
            pltpu.VMEM((group + 2, rows, nz), f32),
            pltpu.VMEM((2, group, rows, nz), f32),
            pltpu.VMEM((2, 2, HALO, rows, nz), f32),
            pltpu.VMEM((2, 2, 2, ngy, ly, nz), f32),
            pltpu.VMEM((3, group, 2, ngy, ly, nz), f32),
            pltpu.VMEM((3, count, lx, ly, nz), f32),
            pltpu.VMEM((count, 128), f32),
            pltpu.VMEM((count, count, 128), f32),
            pltpu.VMEM((count, 128), f32),
            pltpu.VMEM((groups, count, 128), f32),
            dma((3, count)), dma((slots, ngy)), dma((3, count)), dma((slots, ngy)),
            dma((3, 2)), dma((3, 2)), dma((2, count)), dma((2, count)),
            dma((count,)), dma((count,)), dma((groups,)), dma((groups,)),
        ],
        compiler_params=pltpu.CompilerParams(
            collective_id=0, has_side_effects=True, vmem_limit_bytes=32 * 1024 * 1024),
        name="block_step",
    )(rhs, classes, supports)


def solution(mesh):
    ngx, ngy = mesh.shape["gx"], mesh.shape["gy"]
    spread_out = P(None, "gx", "gy", None)
    return jax.shard_map(
        functools.partial(local, ngx, ngy),
        mesh=mesh,
        in_specs=(spread_out, P("gx", "gy", None), P("gx", "gy", None)),
        out_specs=(spread_out, spread_out, spread_out),
        check_vma=False,
    )
```

```python
import functools

import jax
import jax.numpy as jnp
from jax import lax
from jax.experimental import pallas as pl
from jax.experimental.pallas import tpu as pltpu
from jax.sharding import PartitionSpec as P

SPRING = 8.0
OMEGA = 0.6
DAMP = 0.5
HALO = 2

MESH = pl.DeviceIdType.MESH
EXACT = lax.Precision.HIGHEST


def axis_ids(shape, dim):
    return lax.broadcasted_iota(jnp.int32, shape, dim)


def once(f):
    return functools.cache(f)


def halves(u):
    top = u.astype(jnp.bfloat16)
    return top, (u - top.astype(jnp.float32)).astype(jnp.bfloat16)


def kernel(
    ngx, ngy,
    rhs_hbm, classes_hbm, supports_hbm, sol_ref, res_ref, dir_ref,
    rhs_ref, classes_ref, supports_ref,
    mine, cext, rext, scales, weight, spring, cstep, rest, coarse, smooth, first,
    own_c, halo_c, halo_a, fields, returned, part, first_sums, group_sum, last_sums,
    in_sem, gc_send, gc_recv, gr_send, gr_recv, x_send, x_recv, b_send, b_recv, a_send, a_recv, q_send, q_recv,
):
    count, lx, ly, nz = rhs_ref.shape
    group = count // ngy
    groups = ngx // group
    slots = group + 2 * HALO
    rows = ngy * ly
    planes = 2 * slots
    gx, gy = lax.axis_index("gx"), lax.axis_index("gy")
    g, s = gx // group, gx % group
    me = s * ngy + gy
    others = [(me + o) % count for o in range(1, count)]
    other_groups = [(g + o) % groups for o in range(1, groups)]

    loads = [
        pltpu.make_async_copy(classes_hbm, classes_ref, in_sem.at[0]),
        pltpu.make_async_copy(supports_hbm, supports_ref, in_sem.at[1]),
        pltpu.make_async_copy(rhs_hbm, rhs_ref, in_sem.at[2]),
    ]
    for load in loads:
        load.start()

    def member(at_group, j):
        return (at_group * group + j // ngy, j % ngy)

    barrier = pltpu.get_barrier_semaphore()

    def greet(target):
        pl.semaphore_signal(barrier, inc=1, device_id=target, device_id_type=MESH)

    def greet_group(at_group):
        for j in range(count):
            greet(member(at_group, j))

    has_below, has_above = g > 0, g < groups - 1
    for j in others:
        greet(member(g, j))
    pl.when(has_below)(lambda: greet_group(g - 1))
    pl.when(has_above)(lambda: greet_group(g + 1))
    for q in range(groups):
        pl.when(jnp.abs(q - g) > 1)(functools.partial(greet, (q * group + s, gy)))
    below, above = has_below.astype(jnp.int32), has_above.astype(jnp.int32)
    expected = (count - 1) + count * (below + above) + (groups - 1 - below - above)

    def clear(side):
        at = 0 if side == 0 else slots - HALO
        cext[:, at : at + HALO] = jnp.zeros((2, HALO, 2, ngy, ly, nz), jnp.float32)
        rext[at : at + HALO] = jnp.zeros((HALO, 2, ngy, ly, nz), jnp.float32)
        for call in range(2):
            halo_c[call, side] = jnp.zeros((HALO, rows, nz), jnp.float32)
        halo_a[side] = jnp.zeros((2, 2, ngy, ly, nz), jnp.float32)

    pl.when(g == 0)(lambda: clear(0))
    pl.when(g == groups - 1)(lambda: clear(1))
    loads[0].wait()
    density = (classes_ref[...].astype(jnp.float32) + 1.0) / 4.0
    mine[0] = 0.001 + density * density * density
    loads[1].wait()
    mine[1] = supports_ref[...].astype(jnp.float32)
    loads[2].wait()
    pl.semaphore_wait(barrier, expected)

    def coef_copy(dg, j):
        slot = s + HALO - dg * group
        return pltpu.make_async_remote_copy(
            src_ref=mine, dst_ref=cext.at[:, slot, :, gy],
            send_sem=gc_send.at[dg + 1, j], recv_sem=gc_recv.at[slot, gy],
            device_id=member(g + dg, j), device_id_type=MESH)

    def rhs_copy(dg, j):
        slot = s + HALO - dg * group
        return pltpu.make_async_remote_copy(
            src_ref=rhs_ref.at[j], dst_ref=rext.at[slot, :, gy],
            send_sem=gr_send.at[dg + 1, j], recv_sem=gr_recv.at[slot, gy],
            device_id=member(g + dg, j), device_id_type=MESH)

    def outward(action):
        for dg, there in ((-1, has_below), (1, has_above)):
            slot = s + HALO - dg * group

            @pl.when(there & (slot >= 0) & (slot < slots))
            def _():
                for make in (coef_copy, rhs_copy):
                    for j in range(count):
                        action(make(dg, j))

    outward(lambda copy: copy.start())
    for make in (coef_copy, rhs_copy):
        for j in others:
            make(0, j).start()
    cext[:, s + HALO, :, gy] = mine[...]
    rext[s + HALO, :, gy] = rhs_ref[me]

    def wait_coef(slot, y):
        pltpu.make_async_remote_copy(
            src_ref=mine, dst_ref=cext.at[:, slot, :, y], send_sem=gc_send.at[0, 0],
            recv_sem=gc_recv.at[slot, y], device_id=(gx, gy), device_id_type=MESH).wait_recv()

    def wait_rhs(slot, y):
        pltpu.make_async_remote_copy(
            src_ref=rhs_ref.at[0], dst_ref=rext.at[slot, :, y], send_sem=gr_send.at[0, 0],
            recv_sem=gr_recv.at[slot, y], device_id=(gx, gy), device_id_type=MESH).wait_recv()

    def wait_all(wait):
        def side(at):
            for slot in range(at, at + HALO):
                for y in range(ngy):
                    wait(slot, y)

        for j in others:
            wait(HALO + j // ngy, j % ngy)
        pl.when(has_below)(lambda: side(0))
        pl.when(has_above)(lambda: side(HALO + group))

    shape = (rows, nz)
    row_id, lane_id = axis_ids(shape, 0), axis_ids(shape, 1)
    first_row, last_row = row_id == 0, row_id == rows - 1
    first_lane, last_lane = lane_id == 0, lane_id == nz - 1
    tiles = (rows // 8, 8, nz)
    even_row, even_lane = axis_ids(tiles, 1) % 2 == 0, lane_id % 2 == 0

    def before_y(u):
        return jnp.where(first_row, 0.0, pltpu.roll(u, 1, 0))

    def after_y(u):
        return jnp.where(last_row, 0.0, pltpu.roll(u, rows - 1, 0))

    def before_z(u):
        return jnp.where(first_lane, 0.0, pltpu.roll(u, 1, 1))

    def after_z(u):
        return jnp.where(last_lane, 0.0, pltpu.roll(u, nz - 1, 1))

    def pair_sums(u):
        t = u.reshape(tiles)
        t = t + jnp.where(even_row, pltpu.roll(t, 7, 1), pltpu.roll(t, 1, 1))
        u = t.reshape(shape)
        return u + jnp.where(even_lane, pltpu.roll(u, nz - 1, 1), pltpu.roll(u, 1, 1))

    def forward(u):
        back = before_z(u)
        a, d = u + back, u - back
        ab, db = before_y(a), before_y(d)
        return a + ab, a - ab, d + db, d - db

    def inverse(t):
        t00, t10, t01, t11 = t
        ts = (t00 + t10) + after_y(t00 - t10)
        td = (t01 + t11) + after_y(t01 - t11)
        return (ts + td) + after_z(ts - td)

    def element(low, high, i):
        e1, e2, e3 = scales[0, i], scales[1, i], scales[2, i]
        m00 = e1 * (high[0] - low[0])
        s10, d10 = e1 * (high[1] + low[1]), e2 * (high[1] - low[1])
        s01, d01 = e1 * (high[2] + low[2]), e2 * (high[2] - low[2])
        s11, d11 = e2 * (high[3] + low[3]), e3 * (high[3] - low[3])
        return (m00, s10 + d10, s01 + d01, s11 + d11), (-m00, s10 - d10, s01 - d01, s11 - d11)

    def both(low, high, i):
        e1, e2 = scales[0, i], scales[1, i]
        return e1 * (high[1] + low[1]), e1 * (high[2] + low[2]), e2 * (high[3] + low[3])

    def plane_apply(value, start, stop):
        spectrum = once(lambda p: forward(value(p)))
        parts = once(lambda i: element(spectrum(i - 1), spectrum(i), i))
        for p in range(start, stop):
            t = [u + v for u, v in zip(parts(p)[0], parts(p + 1)[1])]
            yield p, inverse(t) + spring[p] * value(p)

    def cell_sums(spectrum, start, stop):
        parts = once(lambda i: element(spectrum(i - 1), spectrum(i), i))
        for cell in range(start, stop):
            p = 2 * cell
            up, down = parts(p)[0], parts(p + 2)[1]
            mid = [2.0 * u for u in both(spectrum(p), spectrum(p + 1), p + 1)]
            t = [up[0] + down[0]] + [up[k + 1] + mid[k] + down[k + 1] for k in range(3)]
            yield cell, inverse(t)

    def coarse_sums(value, start, stop):
        spectrum = once(lambda cell: forward(value(cell)))
        for cell, total in cell_sums(lambda p: spectrum(p // 2), start, stop):
            p = 2 * cell
            yield cell, pair_sums(total + (spring[p] + spring[p + 1]) * value(cell))

    lo, hi = 2 * HALO, planes - 2 * HALO
    near = range(HALO - 1, HALO + group + 1)
    wait_all(wait_coef)

    def inside(p):
        if p < lo:
            return jnp.where(has_below, jnp.float32(1.0), jnp.float32(0.0))
        if p >= hi:
            return jnp.where(has_above, jnp.float32(1.0), jnp.float32(0.0))
        return None

    def shared(amount, value, p):
        there = inside(p)
        return amount / value if there is None else there * (amount / (value + (1.0 - there)))

    def stiff(p):
        return cext[0, p // 2, p % 2].reshape(shape)

    diagonals = {}
    for p in range(lo - 3, hi + 4):
        e = stiff(p)
        scales[0, p] = e * (1.0 / 16.0)
        scales[1, p] = e * (1.0 / 24.0)
        scales[2, p] = e * (1.0 / 48.0)
        if p < hi + 3:
            tied = SPRING * cext[1, p // 2, p % 2].reshape(shape)
            spring[p] = tied
            around = e + stiff(p + 1)
            around = around + after_y(around)
            around = around + after_z(around)
            diagonals[p] = around * (1.0 / 3.0) + tied
            weight[p] = shared(OMEGA, diagonals[p], p)
        if p % 2 and p // 2 in near:
            cstep[p // 2] = shared(DAMP, pair_sums(diagonals[p - 1] + diagonals[p]), p)

    def swap_edges(low_src, high_src, low_dst, high_dst, k):
        down = pltpu.make_async_remote_copy(
            src_ref=low_src, dst_ref=high_dst, send_sem=x_send.at[k, 0], recv_sem=x_recv.at[k, 1],
            device_id=(jnp.maximum(gx - group, 0), gy), device_id_type=MESH)
        up = pltpu.make_async_remote_copy(
            src_ref=high_src, dst_ref=low_dst, send_sem=x_send.at[k, 1], recv_sem=x_recv.at[k, 0],
            device_id=(jnp.minimum(gx + group, ngx - 1), gy), device_id_type=MESH)
        pl.when(has_below)(down.start)
        pl.when(has_above)(up.start)
        return down, up

    def finish_edges(down, up):
        pl.when(has_below)(up.wait_recv)
        pl.when(has_above)(down.wait_recv)

    def drain_edges(down, up):
        pl.when(has_below)(down.wait_send)
        pl.when(has_above)(up.wait_send)

    pending = []

    def correct(source, call):
        def z(p):
            return source(p) * weight[p]

        spectrum = once(lambda p: forward(z(p)))
        for cell, total in cell_sums(spectrum, near.start, near.stop):
            p = 2 * cell
            given = (source(p) - spring[p] * z(p)) + (source(p + 1) - spring[p + 1] * z(p + 1))
            value = pair_sums(given - total)
            rest[cell] = value
            coarse[cell] = cstep[cell] * value
        for cell, total in coarse_sums(lambda c: coarse[c], HALO, HALO + group):
            own_c[call, cell - HALO] = coarse[cell] + cstep[cell] * (rest[cell] - total)
        copies = swap_edges(
            own_c.at[call, pl.ds(0, HALO)], own_c.at[call, pl.ds(group - HALO, HALO)],
            halo_c.at[call, 0], halo_c.at[call, 1], call)
        pending.append(copies)
        finish_edges(*copies)

        def swept(cell):
            if cell < HALO:
                return halo_c[call, 0, cell]
            if cell < HALO + group:
                return own_c[call, cell - HALO]
            return halo_c[call, 1, cell - HALO - group]

        for cell, total in coarse_sums(swept, near.start, near.stop):
            c = swept(cell) + cstep[cell] * (rest[cell] - total)
            for p in (2 * cell, 2 * cell + 1):
                smooth[p] = z(p) + c

    def smoothed(source, start, stop):
        for p, product in plane_apply(lambda p: smooth[p], start, stop):
            yield p, smooth[p] + weight[p] * (source(p) - product)

    def keep(f, p, u):
        fields[f, (p - lo) // 2, (p - lo) % 2] = u.reshape(ngy, ly, nz)

    wait_all(wait_rhs)

    def given_plane(p):
        return rext[p // 2, p % 2].reshape(shape)

    correct(given_plane, 0)
    for p, u in smoothed(given_plane, lo - 1, hi + 1):
        first[p] = u
        if lo <= p < hi:
            keep(0, p, u)
    for p, u in plane_apply(lambda p: first[p], lo, hi):
        keep(1, p, u)

    copies = swap_edges(
        fields.at[1, pl.ds(0, 2)], fields.at[1, pl.ds(group - 2, 2)], halo_a.at[0], halo_a.at[1], 2)
    pending.append(copies)

    def back_copy(k, f, n, j):
        return pltpu.make_async_remote_copy(
            src_ref=fields.at[pl.ds(f, n), j // ngy, :, j % ngy], dst_ref=returned.at[pl.ds(f, n), me],
            send_sem=b_send.at[k, j], recv_sem=b_recv.at[k, me],
            device_id=member(g, j), device_id_type=MESH)

    def wait_back(k, f, n, j):
        pltpu.make_async_remote_copy(
            src_ref=fields.at[pl.ds(f, n), 0, :, 0], dst_ref=returned.at[pl.ds(f, n), j],
            send_sem=b_send.at[k, j], recv_sem=b_recv.at[k, j],
            device_id=(gx, gy), device_id_type=MESH).wait_recv()

    def send_back(k, f, n):
        for j in others:
            back_copy(k, f, n, j).start()
        for i in range(f, f + n):
            returned[i, me] = fields[i, s, :, gy]

    send_back(0, 0, 2)
    finish_edges(*copies)

    def product_plane(p):
        if p < lo:
            u = halo_a[0, p // 2, p % 2]
        elif p < hi:
            u = fields[1, (p - lo) // 2, (p - lo) % 2]
        else:
            u = halo_a[1, (p - hi) // 2, (p - hi) % 2]
        return u.reshape(shape)

    correct(product_plane, 1)
    for p, u in smoothed(product_plane, lo, hi):
        keep(2, p, u)
    send_back(1, 2, 1)

    def flat(block):
        parts = []
        for a in range(lx):
            turned = jnp.swapaxes(block[:, a], 0, 1)
            parts += [turned[b] for b in range(ly)]
        return jnp.concatenate(parts, axis=1)

    given = flat(rhs_ref[...])
    for j in others:
        wait_back(0, 0, 2, j)
    field, product = flat(returned[0]), flat(returned[1])
    for j in others:
        wait_back(1, 2, 1, j)
    twice = flat(returned[2])

    def dot(left, right, dims):
        return lax.dot_general(left, right, (dims, ((), ())), preferred_element_type=jnp.float32)

    left_top, left_low = halves(jnp.concatenate([field, product], axis=0))
    right_top, right_low = halves(jnp.concatenate([product, given, field, twice], axis=0))
    sums = dot(
        jnp.concatenate([left_top, left_low, left_top], axis=1),
        jnp.concatenate([right_top, right_top, right_low], axis=1), ((1,), (1,)))
    wide = 4 * count
    lane = axis_ids((count, wide), 1)
    part[...] = jnp.zeros_like(part)
    part[:, 0:wide] = jnp.where(lane < 2 * count, sums[:count], sums[count:])

    def sum_copy(j):
        return pltpu.make_async_remote_copy(
            src_ref=part, dst_ref=first_sums.at[me], send_sem=a_send.at[j], recv_sem=a_recv.at[me],
            device_id=member(g, j), device_id_type=MESH)

    def sum_wait(j):
        pltpu.make_async_remote_copy(
            src_ref=part, dst_ref=first_sums.at[j], send_sem=a_send.at[j], recv_sem=a_recv.at[j],
            device_id=(gx, gy), device_id_type=MESH).wait_recv()

    for j in others:
        sum_copy(j).start()
    first_sums[me] = part[...]
    for j in others:
        sum_wait(j)
    group_sum[...] = jnp.sum(first_sums[...], axis=0)

    def total_copy(q):
        return pltpu.make_async_remote_copy(
            src_ref=group_sum, dst_ref=last_sums.at[g], send_sem=q_send.at[q], recv_sem=q_recv.at[g],
            device_id=(q * group + s, gy), device_id_type=MESH)

    def total_wait(q):
        pltpu.make_async_remote_copy(
            src_ref=group_sum, dst_ref=last_sums.at[q], send_sem=q_send.at[q], recv_sem=q_recv.at[q],
            device_id=(gx, gy), device_id_type=MESH).wait_recv()

    for q in other_groups:
        total_copy(q).start()
    last_sums[g] = group_sum[...]
    for q in other_groups:
        total_wait(q)
    system = jnp.sum(last_sums[...], axis=0)

    lane = axis_ids(system.shape, 1)
    row = axis_ids(system.shape, 0)
    mirrored = pltpu.roll(system, system.shape[1] - 2 * count, 1)
    system = jnp.where(lane < count, 0.5 * (system + mirrored), system)
    for k in range(count):
        column = jnp.sum(jnp.where(lane == k, system, 0.0), axis=1, keepdims=True)
        pivot_row = system[k : k + 1]
        scaled = pivot_row / pivot_row[:, k : k + 1]
        system = jnp.where(row == k, scaled, system - column * scaled)

    def columns(n):
        return system[:, n * count : (n + 1) * count]

    step = columns(1)
    turn = jnp.dot(columns(3), step, precision=EXACT, preferred_element_type=jnp.float32) - columns(2)

    def mixed(coef, u):
        coef_top, u_top = [v.astype(jnp.bfloat16).astype(jnp.float32) for v in (coef, u)]
        coefs = jnp.concatenate([coef_top, coef - coef_top, coef_top], axis=0).astype(jnp.bfloat16)
        terms = jnp.concatenate([u_top, u_top, u - u_top], axis=0).astype(jnp.bfloat16)
        return dot(coefs, terms, ((0,), (0,)))

    def put(ref, u):
        for a in range(lx):
            at = a * ly
            block = jnp.stack([u[:, (at + b) * nz : (at + b + 1) * nz] for b in range(ly)], axis=0)
            ref[:, a] = jnp.swapaxes(block, 0, 1)

    put(sol_ref, mixed(step, field))
    put(res_ref, given - mixed(step, product))
    put(dir_ref, field + mixed(jnp.concatenate([turn, -step], axis=0), jnp.concatenate([field, twice], axis=0)))

    outward(lambda copy: copy.wait_send())
    for make in (coef_copy, rhs_copy):
        for j in others:
            make(0, j).wait_send()
    for copies in pending:
        drain_edges(*copies)
    for k, f, n in ((0, 0, 2), (1, 2, 1)):
        for j in others:
            back_copy(k, f, n, j).wait_send()
    for j in others:
        sum_copy(j).wait_send()
    for q in other_groups:
        total_copy(q).wait_send()


def local(ngx, ngy, rhs, classes, supports):
    count, lx, ly, nz = rhs.shape
    group = count // ngy
    groups = ngx // group
    slots = group + 2 * HALO
    rows = ngy * ly
    planes = 2 * slots
    f32 = jnp.float32
    dma = pltpu.SemaphoreType.DMA
    return pl.pallas_call(
        functools.partial(kernel, ngx, ngy),
        out_shape=[jax.ShapeDtypeStruct(rhs.shape, f32)] * 3,
        in_specs=[pl.BlockSpec(memory_space=pltpu.HBM)] * 3,
        out_specs=[pl.BlockSpec(memory_space=pltpu.VMEM)] * 3,
        scratch_shapes=[
            pltpu.VMEM(rhs.shape, f32),
            pltpu.VMEM(classes.shape, jnp.int32),
            pltpu.VMEM(supports.shape, jnp.int32),
            pltpu.VMEM((2, lx, ly, nz), f32),
            pltpu.VMEM((2, slots, 2, ngy, ly, nz), f32),
            pltpu.VMEM((slots, 2, ngy, ly, nz), f32),
            pltpu.VMEM((3, planes, rows, nz), f32),
            pltpu.VMEM((planes, rows, nz), f32),
            pltpu.VMEM((planes, rows, nz), f32),
            pltpu.VMEM((slots, rows, nz), f32),
            pltpu.VMEM((slots, rows, nz), f32),
            pltpu.VMEM((slots, rows, nz), f32),
            pltpu.VMEM((planes, rows, nz), f32),
            pltpu.VMEM((planes, rows, nz), f32),
            pltpu.VMEM((2, group, rows, nz), f32),
            pltpu.VMEM((2, 2, HALO, rows, nz), f32),
            pltpu.VMEM((2, 2, 2, ngy, ly, nz), f32),
            pltpu.VMEM((3, group, 2, ngy, ly, nz), f32),
            pltpu.VMEM((3, count, lx, ly, nz), f32),
            pltpu.VMEM((count, 128), f32),
            pltpu.VMEM((count, count, 128), f32),
            pltpu.VMEM((count, 128), f32),
            pltpu.VMEM((groups, count, 128), f32),
            dma((3,)), dma((3, count)), dma((slots, ngy)), dma((3, count)), dma((slots, ngy)),
            dma((3, 2)), dma((3, 2)), dma((2, count)), dma((2, count)),
            dma((count,)), dma((count,)), dma((groups,)), dma((groups,)),
        ],
        compiler_params=pltpu.CompilerParams(
            collective_id=0, has_side_effects=True, vmem_limit_bytes=32 * 1024 * 1024),
        name="block_step",
    )(rhs, classes, supports)


def solution(mesh):
    ngx, ngy = mesh.shape["gx"], mesh.shape["gy"]
    spread_out = P(None, "gx", "gy", None)
    return jax.shard_map(
        functools.partial(local, ngx, ngy),
        mesh=mesh,
        in_specs=(spread_out, P("gx", "gy", None), P("gx", "gy", None)),
        out_specs=(spread_out, spread_out, spread_out),
        check_vma=False,
    )
```

```python
import functools

import jax
import jax.numpy as jnp
from jax import lax
from jax.experimental import pallas as pl
from jax.experimental.pallas import tpu as pltpu
from jax.sharding import PartitionSpec as P

SPRING = 8.0
OMEGA = 0.6
DAMP = 0.5
HALO = 2

DIRECT = 64

MESH = pl.DeviceIdType.MESH
EXACT = lax.Precision.HIGHEST


def axis_ids(shape, dim):
    return lax.broadcasted_iota(jnp.int32, shape, dim)


def once(f):
    return functools.cache(f)


def kernel(
    ngx, ngy,
    rhs_hbm, classes_hbm, supports_hbm, sol_hbm, res_hbm, dir_hbm,
    classes_ref, supports_ref, outs,
    pack, ext, scales, weight, spring, cstep, rest, coarse, smooth, first,
    own_c, halo_c, halo_a, fields, returned, part, first_sums, group_sum, last_sums,
    in_sem, out_sem, g_send, g_recv, x_send, x_recv, b_send, b_recv, a_send, a_recv, q_send, q_recv,
):
    count, lx, ly, nz = rhs_hbm.shape
    group = count // ngy
    groups = ngx // group
    slots = group + 2 * HALO
    rows = ngy * ly
    planes = 2 * slots
    gx, gy = lax.axis_index("gx"), lax.axis_index("gy")
    g, s = gx // group, gx % group
    me = s * ngy + gy
    others = [(me + o) % count for o in range(1, count)]
    other_groups = [(g + o) % groups for o in range(1, groups)]

    devices = ngx * ngy
    direct = devices <= DIRECT
    place = gx * ngy + gy
    team, seat = (devices, place) if direct else (count, me)
    teammates = [(seat + o) % team for o in range(1, team)]

    loads = [
        pltpu.make_async_copy(classes_hbm, classes_ref, in_sem.at[0]),
        pltpu.make_async_copy(supports_hbm, supports_ref, in_sem.at[1]),
        pltpu.make_async_copy(rhs_hbm, pack.at[:, 0], in_sem.at[2]),
    ]
    for load in loads:
        load.start()

    def member(at_group, j):
        return (at_group * group + j // ngy, j % ngy)

    barrier = pltpu.get_barrier_semaphore()

    def greet(target):
        pl.semaphore_signal(barrier, inc=1, device_id=target, device_id_type=MESH)

    def greet_group(at_group):
        for j in range(count):
            greet(member(at_group, j))

    has_below, has_above = g > 0, g < groups - 1
    if direct:
        for t in teammates:
            greet((t // ngy, t % ngy))
        expected = devices - 1
    else:
        for j in others:
            greet(member(g, j))
        pl.when(has_below)(lambda: greet_group(g - 1))
        pl.when(has_above)(lambda: greet_group(g + 1))
        for q in range(groups):
            pl.when(jnp.abs(q - g) > 1)(functools.partial(greet, (q * group + s, gy)))
        below, above = has_below.astype(jnp.int32), has_above.astype(jnp.int32)
        expected = (count - 1) + count * (below + above) + (groups - 1 - below - above)

    def clear(side):
        at = 0 if side == 0 else slots - HALO
        ext[:, at : at + HALO] = jnp.zeros((3, HALO, 2, ngy, ly, nz), jnp.float32)
        for call in range(2):
            halo_c[call, side] = jnp.zeros((HALO, rows, nz), jnp.float32)
        halo_a[side] = jnp.zeros((2, 2, ngy, ly, nz), jnp.float32)

    pl.when(g == 0)(lambda: clear(0))
    pl.when(g == groups - 1)(lambda: clear(1))
    loads[0].wait()
    density = (classes_ref[...].astype(jnp.float32) + 1.0) / 4.0
    stiff_own = 0.001 + density * density * density
    loads[1].wait()
    support_own = supports_ref[...].astype(jnp.float32)
    for j in range(count):
        pack[j, 1] = stiff_own
        pack[j, 2] = support_own
    loads[2].wait()
    pl.semaphore_wait(barrier, expected)

    def gather_copy(dg, j):
        slot = s + HALO - dg * group
        return pltpu.make_async_remote_copy(
            src_ref=pack.at[j], dst_ref=ext.at[:, slot, :, gy],
            send_sem=g_send.at[dg + 1, j], recv_sem=g_recv.at[slot, gy],
            device_id=member(g + dg, j), device_id_type=MESH)

    def outward(action):
        for dg, there in ((-1, has_below), (1, has_above)):
            slot = s + HALO - dg * group

            @pl.when(there & (slot >= 0) & (slot < slots))
            def _():
                for j in range(count):
                    action(gather_copy(dg, j))

    outward(lambda copy: copy.start())
    for j in others:
        gather_copy(0, j).start()
    ext[:, s + HALO, :, gy] = pack[me]

    def wait_slab(slot, y):
        pltpu.make_async_remote_copy(
            src_ref=pack.at[0], dst_ref=ext.at[:, slot, :, y], send_sem=g_send.at[0, 0],
            recv_sem=g_recv.at[slot, y], device_id=(gx, gy), device_id_type=MESH).wait_recv()

    def wait_side(at):
        for slot in range(at, at + HALO):
            for y in range(ngy):
                wait_slab(slot, y)

    shape = (rows, nz)
    row_id, lane_id = axis_ids(shape, 0), axis_ids(shape, 1)
    first_row, last_row = row_id == 0, row_id == rows - 1
    first_lane, last_lane = lane_id == 0, lane_id == nz - 1
    tiles = (rows // 8, 8, nz)
    even_row, even_lane = axis_ids(tiles, 1) % 2 == 0, lane_id % 2 == 0

    def before_y(u):
        return jnp.where(first_row, 0.0, pltpu.roll(u, 1, 0))

    def after_y(u):
        return jnp.where(last_row, 0.0, pltpu.roll(u, rows - 1, 0))

    def before_z(u):
        return jnp.where(first_lane, 0.0, pltpu.roll(u, 1, 1))

    def after_z(u):
        return jnp.where(last_lane, 0.0, pltpu.roll(u, nz - 1, 1))

    def pair_sums(u):
        t = u.reshape(tiles)
        t = t + jnp.where(even_row, pltpu.roll(t, 7, 1), pltpu.roll(t, 1, 1))
        u = t.reshape(shape)
        return u + jnp.where(even_lane, pltpu.roll(u, nz - 1, 1), pltpu.roll(u, 1, 1))

    def forward(u):
        back = before_z(u)
        a, d = u + back, u - back
        ab, db = before_y(a), before_y(d)
        return a + ab, a - ab, d + db, d - db

    def inverse(t):
        t00, t10, t01, t11 = t
        ts = (t00 + t10) + after_y(t00 - t10)
        td = (t01 + t11) + after_y(t01 - t11)
        return (ts + td) + after_z(ts - td)

    def element(low, high, i):
        e1, e2, e3 = scales[0, i], scales[1, i], scales[2, i]
        m00 = e1 * (high[0] - low[0])
        s10, d10 = e1 * (high[1] + low[1]), e2 * (high[1] - low[1])
        s01, d01 = e1 * (high[2] + low[2]), e2 * (high[2] - low[2])
        s11, d11 = e2 * (high[3] + low[3]), e3 * (high[3] - low[3])
        return (m00, s10 + d10, s01 + d01, s11 + d11), (-m00, s10 - d10, s01 - d01, s11 - d11)

    def both(low, high, i):
        e1, e2 = scales[0, i], scales[1, i]
        return e1 * (high[1] + low[1]), e1 * (high[2] + low[2]), e2 * (high[3] + low[3])

    def plane_apply(value, start, stop):
        spectrum = once(lambda p: forward(value(p)))
        parts = once(lambda i: element(spectrum(i - 1), spectrum(i), i))
        for p in range(start, stop):
            t = [u + v for u, v in zip(parts(p)[0], parts(p + 1)[1])]
            yield p, inverse(t) + spring[p] * value(p)

    def cell_sums(spectrum, start, stop):
        parts = once(lambda i: element(spectrum(i - 1), spectrum(i), i))
        for cell in range(start, stop):
            p = 2 * cell
            up, down = parts(p)[0], parts(p + 2)[1]
            mid = [2.0 * u for u in both(spectrum(p), spectrum(p + 1), p + 1)]
            t = [up[0] + down[0]] + [up[k + 1] + mid[k] + down[k + 1] for k in range(3)]
            yield cell, inverse(t)

    def coarse_sums(value, start, stop):
        spectrum = once(lambda cell: forward(value(cell)))
        for cell, total in cell_sums(lambda p: spectrum(p // 2), start, stop):
            p = 2 * cell
            yield cell, pair_sums(total + (spring[p] + spring[p + 1]) * value(cell))

    lo, hi = 2 * HALO, planes - 2 * HALO
    near = range(HALO - 1, HALO + group + 1)
    for j in others:
        wait_slab(HALO + j // ngy, j % ngy)
    pl.when(has_below)(lambda: wait_side(0))
    pl.when(has_above)(lambda: wait_side(HALO + group))

    def inside(p):
        if p < lo:
            return jnp.where(has_below, jnp.float32(1.0), jnp.float32(0.0))
        if p >= hi:
            return jnp.where(has_above, jnp.float32(1.0), jnp.float32(0.0))
        return None

    def shared(amount, value, p):
        there = inside(p)
        return amount / value if there is None else there * (amount / (value + (1.0 - there)))

    def stiff(p):
        return ext[1, p // 2, p % 2].reshape(shape)

    diagonals = {}
    for p in range(lo - 3, hi + 4):
        e = stiff(p)
        scales[0, p] = e * (1.0 / 16.0)
        scales[1, p] = e * (1.0 / 24.0)
        scales[2, p] = e * (1.0 / 48.0)
        if p < hi + 3:
            tied = SPRING * ext[2, p // 2, p % 2].reshape(shape)
            spring[p] = tied
            around = e + stiff(p + 1)
            around = around + after_y(around)
            around = around + after_z(around)
            diagonals[p] = around * (1.0 / 3.0) + tied
            weight[p] = shared(OMEGA, diagonals[p], p)
        if p % 2 and p // 2 in near:
            cstep[p // 2] = shared(DAMP, pair_sums(diagonals[p - 1] + diagonals[p]), p)

    def swap_edges(low_src, high_src, low_dst, high_dst, k):
        down = pltpu.make_async_remote_copy(
            src_ref=low_src, dst_ref=high_dst, send_sem=x_send.at[k, 0], recv_sem=x_recv.at[k, 1],
            device_id=(jnp.maximum(gx - group, 0), gy), device_id_type=MESH)
        up = pltpu.make_async_remote_copy(
            src_ref=high_src, dst_ref=low_dst, send_sem=x_send.at[k, 1], recv_sem=x_recv.at[k, 0],
            device_id=(jnp.minimum(gx + group, ngx - 1), gy), device_id_type=MESH)
        pl.when(has_below)(down.start)
        pl.when(has_above)(up.start)
        return down, up

    def finish_edges(down, up):
        pl.when(has_below)(up.wait_recv)
        pl.when(has_above)(down.wait_recv)

    def drain_edges(down, up):
        pl.when(has_below)(down.wait_send)
        pl.when(has_above)(up.wait_send)

    pending = []

    def correct(source, call, meanwhile=lambda: None):
        def z(p):
            return source(p) * weight[p]

        spectrum = once(lambda p: forward(z(p)))
        for cell, total in cell_sums(spectrum, near.start, near.stop):
            p = 2 * cell
            given = (source(p) - spring[p] * z(p)) + (source(p + 1) - spring[p + 1] * z(p + 1))
            value = pair_sums(given - total)
            rest[cell] = value
            coarse[cell] = cstep[cell] * value
        for cell, total in coarse_sums(lambda c: coarse[c], HALO, HALO + group):
            own_c[call, cell - HALO] = coarse[cell] + cstep[cell] * (rest[cell] - total)
        copies = swap_edges(
            own_c.at[call, pl.ds(0, HALO)], own_c.at[call, pl.ds(group - HALO, HALO)],
            halo_c.at[call, 0], halo_c.at[call, 1], call)
        pending.append(copies)
        meanwhile()
        finish_edges(*copies)

        def swept(cell):
            if cell < HALO:
                return halo_c[call, 0, cell]
            if cell < HALO + group:
                return own_c[call, cell - HALO]
            return halo_c[call, 1, cell - HALO - group]

        for cell, total in coarse_sums(swept, near.start, near.stop):
            c = swept(cell) + cstep[cell] * (rest[cell] - total)
            for p in (2 * cell, 2 * cell + 1):
                smooth[p] = z(p) + c

    def smoothed(source, start, stop):
        for p, product in plane_apply(lambda p: smooth[p], start, stop):
            yield p, smooth[p] + weight[p] * (source(p) - product)

    def keep(f, p, u):
        fields[f, (p - lo) // 2, (p - lo) % 2] = u.reshape(ngy, ly, nz)

    def given_plane(p):
        return ext[0, p // 2, p % 2].reshape(shape)

    correct(given_plane, 0)
    for p, u in smoothed(given_plane, lo - 1, hi + 1):
        first[p] = u
        if lo <= p < hi:
            keep(0, p, u)
    for p, u in plane_apply(lambda p: first[p], lo, hi):
        keep(1, p, u)

    copies = swap_edges(
        fields.at[1, pl.ds(0, 2)], fields.at[1, pl.ds(group - 2, 2)], halo_a.at[0], halo_a.at[1], 2)
    pending.append(copies)

    def back_copy(k, f, n, j):
        return pltpu.make_async_remote_copy(
            src_ref=fields.at[pl.ds(f, n), j // ngy, :, j % ngy], dst_ref=returned.at[pl.ds(f, n), me],
            send_sem=b_send.at[k, j], recv_sem=b_recv.at[k, me],
            device_id=member(g, j), device_id_type=MESH)

    def wait_back(k, f, n, j):
        pltpu.make_async_remote_copy(
            src_ref=fields.at[pl.ds(f, n), 0, :, 0], dst_ref=returned.at[pl.ds(f, n), j],
            send_sem=b_send.at[k, j], recv_sem=b_recv.at[k, j],
            device_id=(gx, gy), device_id_type=MESH).wait_recv()

    def send_back(k, f, n):
        for j in others:
            back_copy(k, f, n, j).start()
        for i in range(f, f + n):
            returned[i, me] = fields[i, s, :, gy]

    send_back(0, 0, 2)
    finish_edges(*copies)

    def product_plane(p):
        if p < lo:
            u = halo_a[0, p // 2, p % 2]
        elif p < hi:
            u = fields[1, (p - lo) // 2, (p - lo) % 2]
        else:
            u = halo_a[1, (p - hi) // 2, (p - hi) % 2]
        return u.reshape(shape)

    def sum_copy(k, t):
        to = (t // ngy, t % ngy) if direct else member(g, t)
        return pltpu.make_async_remote_copy(
            src_ref=part.at[k], dst_ref=first_sums.at[k, seat], send_sem=a_send.at[k, t],
            recv_sem=a_recv.at[k, seat], device_id=to, device_id_type=MESH)

    def sum_wait(k, t):
        pltpu.make_async_remote_copy(
            src_ref=part.at[k], dst_ref=first_sums.at[k, t], send_sem=a_send.at[k, t],
            recv_sem=a_recv.at[k, t], device_id=(gx, gy), device_id_type=MESH).wait_recv()

    def total_copy(k, q):
        return pltpu.make_async_remote_copy(
            src_ref=group_sum.at[k], dst_ref=last_sums.at[k, g], send_sem=q_send.at[k, q],
            recv_sem=q_recv.at[k, g], device_id=(q * group + s, gy), device_id_type=MESH)

    def total_wait(k, q):
        pltpu.make_async_remote_copy(
            src_ref=group_sum.at[k], dst_ref=last_sums.at[k, q], send_sem=q_send.at[k, q],
            recv_sem=q_recv.at[k, q], device_id=(gx, gy), device_id_type=MESH).wait_recv()

    def start_sum(k, value):
        part[k] = jnp.zeros((count, 128), jnp.float32)
        part[k, :, 0 : value.shape[1]] = value
        for t in teammates:
            sum_copy(k, t).start()
        first_sums[k, seat] = part[k]

    def finish_sum(k):
        for t in teammates:
            sum_wait(k, t)
        total = jnp.sum(first_sums[k], axis=0)
        if direct:
            return total
        group_sum[k] = total
        for q in other_groups:
            total_copy(k, q).start()
        last_sums[k, g] = group_sum[k]
        for q in other_groups:
            total_wait(k, q)
        return jnp.sum(last_sums[k], axis=0)

    def flat(block):
        parts = []
        for a in range(lx):
            turned = jnp.swapaxes(block[:, a], 0, 1)
            parts += [turned[b] for b in range(ly)]
        return jnp.concatenate(parts, axis=1)

    def dot(left, right, dims):
        return lax.dot_general(
            left, right, (dims, ((), ())), precision=EXACT, preferred_element_type=jnp.float32)

    def first_products():
        for j in others:
            wait_back(0, 0, 2, j)
        field, product, given = flat(returned[0]), flat(returned[1]), flat(pack[:, 0])
        start_sum(0, dot(field, jnp.concatenate([product, given], axis=0), ((1,), (1,))))

    correct(product_plane, 1, first_products)
    for p, u in smoothed(product_plane, lo, hi):
        keep(2, p, u)
    send_back(1, 2, 1)

    field, product, given = flat(returned[0]), flat(returned[1]), flat(pack[:, 0])
    system = finish_sum(0)

    lane = axis_ids(system.shape, 1)
    row = axis_ids(system.shape, 0)
    crossed = jnp.transpose(system[:, 0:count])
    square = 0.5 * (system[:, 0:count] + crossed)
    same = axis_ids((count, count), 0) == axis_ids((count, count), 1)
    unit = jnp.where(same, 1.0, 0.0)
    rest_of = jnp.zeros((count, 128 - 4 * count), jnp.float32)
    system = jnp.concatenate([square, system[:, count : 2 * count], crossed, unit, rest_of], axis=1)
    for k in range(count):
        column = jnp.sum(jnp.where(lane == k, system, 0.0), axis=1, keepdims=True)
        pivot_row = system[k : k + 1]
        scaled = pivot_row / pivot_row[:, k : k + 1]
        system = jnp.where(row == k, scaled, system - column * scaled)

    def columns(n):
        return system[:, n * count : (n + 1) * count]

    step, turned_field, inverse_square = columns(1), columns(2), columns(3)

    def mixed(coef, u):
        return dot(coef, u, ((0,), (0,)))

    stores = []

    def put(n, target, u):
        for a in range(lx):
            at = a * ly
            block = jnp.stack([u[:, (at + b) * nz : (at + b + 1) * nz] for b in range(ly)], axis=0)
            outs[n, :, a] = jnp.swapaxes(block, 0, 1)
        stores.append(pltpu.make_async_copy(outs.at[n], target, out_sem.at[n]))
        stores[-1].start()

    put(0, sol_hbm, mixed(step, field))
    put(1, res_hbm, given - mixed(step, product))

    for j in others:
        wait_back(1, 2, 1, j)
    twice = flat(returned[2])
    start_sum(1, dot(product, twice, ((1,), (1,))))
    base = field - mixed(step, twice)
    second = finish_sum(1)[:, 0:count]

    def times(a, b):
        return jnp.dot(a, b, precision=EXACT, preferred_element_type=jnp.float32)

    turn = times(inverse_square, times(second, step)) - turned_field
    put(2, dir_hbm, base + mixed(turn, field))

    outward(lambda copy: copy.wait_send())
    for j in others:
        gather_copy(0, j).wait_send()
    for copies in pending:
        drain_edges(*copies)
    for k, f, n in ((0, 0, 2), (1, 2, 1)):
        for j in others:
            back_copy(k, f, n, j).wait_send()
    for k in range(2):
        for t in teammates:
            sum_copy(k, t).wait_send()
        if not direct:
            for q in other_groups:
                total_copy(k, q).wait_send()
    for store in stores:
        store.wait()


def local(ngx, ngy, rhs, classes, supports):
    count, lx, ly, nz = rhs.shape
    group = count // ngy
    groups = ngx // group
    slots = group + 2 * HALO
    rows = ngy * ly
    planes = 2 * slots
    team = ngx * ngy if ngx * ngy <= DIRECT else count
    f32 = jnp.float32
    dma = pltpu.SemaphoreType.DMA
    return pl.pallas_call(
        functools.partial(kernel, ngx, ngy),
        out_shape=[jax.ShapeDtypeStruct(rhs.shape, f32)] * 3,
        in_specs=[pl.BlockSpec(memory_space=pltpu.HBM)] * 3,
        out_specs=[pl.BlockSpec(memory_space=pltpu.HBM)] * 3,
        scratch_shapes=[
            pltpu.VMEM(classes.shape, jnp.int32),
            pltpu.VMEM(supports.shape, jnp.int32),
            pltpu.VMEM((3, count, lx, ly, nz), f32),
            pltpu.VMEM((count, 3, lx, ly, nz), f32),
            pltpu.VMEM((3, slots, 2, ngy, ly, nz), f32),
            pltpu.VMEM((3, planes, rows, nz), f32),
            pltpu.VMEM((planes, rows, nz), f32),
            pltpu.VMEM((planes, rows, nz), f32),
            pltpu.VMEM((slots, rows, nz), f32),
            pltpu.VMEM((slots, rows, nz), f32),
            pltpu.VMEM((slots, rows, nz), f32),
            pltpu.VMEM((planes, rows, nz), f32),
            pltpu.VMEM((planes, rows, nz), f32),
            pltpu.VMEM((2, group, rows, nz), f32),
            pltpu.VMEM((2, 2, HALO, rows, nz), f32),
            pltpu.VMEM((2, 2, 2, ngy, ly, nz), f32),
            pltpu.VMEM((3, group, 2, ngy, ly, nz), f32),
            pltpu.VMEM((3, count, lx, ly, nz), f32),
            pltpu.VMEM((2, count, 128), f32),
            pltpu.VMEM((2, team, count, 128), f32),
            pltpu.VMEM((2, count, 128), f32),
            pltpu.VMEM((2, groups, count, 128), f32),
            dma((3,)), dma((3,)), dma((3, count)), dma((slots, ngy)),
            dma((3, 2)), dma((3, 2)), dma((2, count)), dma((2, count)),
            dma((2, team)), dma((2, team)), dma((2, groups)), dma((2, groups)),
        ],
        compiler_params=pltpu.CompilerParams(
            collective_id=0, has_side_effects=True),
        name="block_step",
    )(rhs, classes, supports)


def solution(mesh):
    ngx, ngy = mesh.shape["gx"], mesh.shape["gy"]
    spread_out = P(None, "gx", "gy", None)
    return jax.shard_map(
        functools.partial(local, ngx, ngy),
        mesh=mesh,
        in_specs=(spread_out, P("gx", "gy", None), P("gx", "gy", None)),
        out_specs=(spread_out, spread_out, spread_out),
        check_vma=False,
    )
```

```python
import functools

import jax
import jax.numpy as jnp
from jax import lax
from jax.experimental import pallas as pl
from jax.experimental.pallas import tpu as pltpu
from jax.sharding import PartitionSpec as P

SPRING = 8.0
OMEGA = 0.6
DAMP = 0.5
HALO = 2

DIRECT = 0

MESH = pl.DeviceIdType.MESH
EXACT = lax.Precision.HIGHEST


def axis_ids(shape, dim):
    return lax.broadcasted_iota(jnp.int32, shape, dim)


def once(f):
    return functools.cache(f)


def kernel(
    ngx, ngy,
    rhs_hbm, classes_hbm, supports_hbm, sol_hbm, res_hbm, dir_hbm,
    classes_ref, supports_ref, outs,
    flats, pack, ext, scales, weight, spring, cstep, rest, coarse, smooth, first,
    own_c, halo_c, halo_a, fields, returned, part, first_sums, group_sum, last_sums,
    in_sem, out_sem, g_send, g_recv, x_send, x_recv, b_send, b_recv, a_send, a_recv, q_send, q_recv,
):
    count, lx, ly, nz = rhs_hbm.shape
    group = count // ngy
    groups = ngx // group
    slots = group + 2 * HALO
    rows = ngy * ly
    planes = 2 * slots
    gx, gy = lax.axis_index("gx"), lax.axis_index("gy")
    g, s = gx // group, gx % group
    me = s * ngy + gy
    others = [(me + o) % count for o in range(1, count)]
    other_groups = [(g + o) % groups for o in range(1, groups)]

    devices = ngx * ngy
    direct = devices <= DIRECT
    place = gx * ngy + gy
    team, seat = (devices, place) if direct else (count, me)
    teammates = [(seat + o) % team for o in range(1, team)]

    loads = [
        pltpu.make_async_copy(classes_hbm, classes_ref, in_sem.at[0]),
        pltpu.make_async_copy(supports_hbm, supports_ref, in_sem.at[1]),
        pltpu.make_async_copy(rhs_hbm, pack.at[:, 0], in_sem.at[2]),
    ]
    for load in loads:
        load.start()

    def member(at_group, j):
        return (at_group * group + j // ngy, j % ngy)

    barrier = pltpu.get_barrier_semaphore()

    def greet(target):
        pl.semaphore_signal(barrier, inc=1, device_id=target, device_id_type=MESH)

    def greet_group(at_group):
        for j in range(count):
            greet(member(at_group, j))

    has_below, has_above = g > 0, g < groups - 1
    if direct:
        for t in teammates:
            greet((t // ngy, t % ngy))
        expected = devices - 1
    else:
        for j in others:
            greet(member(g, j))
        pl.when(has_below)(lambda: greet_group(g - 1))
        pl.when(has_above)(lambda: greet_group(g + 1))
        for q in range(groups):
            pl.when(jnp.abs(q - g) > 1)(functools.partial(greet, (q * group + s, gy)))
        below, above = has_below.astype(jnp.int32), has_above.astype(jnp.int32)
        expected = (count - 1) + count * (below + above) + (groups - 1 - below - above)

    def clear(side):
        at = 0 if side == 0 else slots - HALO
        ext[:, at : at + HALO] = jnp.zeros((3, HALO, 2, ngy, ly, nz), jnp.float32)
        for call in range(2):
            halo_c[call, side] = jnp.zeros((HALO, rows, nz), jnp.float32)
        halo_a[side] = jnp.zeros((2, 2, ngy, ly, nz), jnp.float32)

    pl.when(g == 0)(lambda: clear(0))
    pl.when(g == groups - 1)(lambda: clear(1))
    loads[0].wait()
    density = (classes_ref[...].astype(jnp.float32) + 1.0) / 4.0
    stiff_own = 0.001 + density * density * density
    loads[1].wait()
    support_own = supports_ref[...].astype(jnp.float32)
    for j in range(count):
        pack[j, 1] = stiff_own
        pack[j, 2] = support_own
    loads[2].wait()
    pl.semaphore_wait(barrier, expected)

    def gather_copy(dg, j):
        slot = s + HALO - dg * group
        return pltpu.make_async_remote_copy(
            src_ref=pack.at[j], dst_ref=ext.at[:, slot, :, gy],
            send_sem=g_send.at[dg + 1, j], recv_sem=g_recv.at[slot, gy],
            device_id=member(g + dg, j), device_id_type=MESH)

    def outward(action):
        for dg, there in ((-1, has_below), (1, has_above)):
            slot = s + HALO - dg * group

            @pl.when(there & (slot >= 0) & (slot < slots))
            def _():
                for j in range(count):
                    action(gather_copy(dg, j))

    outward(lambda copy: copy.start())
    for j in others:
        gather_copy(0, j).start()
    ext[:, s + HALO, :, gy] = pack[me]

    def wait_slab(slot, y):
        pltpu.make_async_remote_copy(
            src_ref=pack.at[0], dst_ref=ext.at[:, slot, :, y], send_sem=g_send.at[0, 0],
            recv_sem=g_recv.at[slot, y], device_id=(gx, gy), device_id_type=MESH).wait_recv()

    def wait_side(at):
        for slot in range(at, at + HALO):
            for y in range(ngy):
                wait_slab(slot, y)

    shape = (rows, nz)
    row_id, lane_id = axis_ids(shape, 0), axis_ids(shape, 1)
    first_row, last_row = row_id == 0, row_id == rows - 1
    first_lane, last_lane = lane_id == 0, lane_id == nz - 1
    tiles = (rows // 8, 8, nz)
    even_row, even_lane = axis_ids(tiles, 1) % 2 == 0, lane_id % 2 == 0

    def before_y(u):
        return jnp.where(first_row, 0.0, pltpu.roll(u, 1, 0))

    def after_y(u):
        return jnp.where(last_row, 0.0, pltpu.roll(u, rows - 1, 0))

    def before_z(u):
        return jnp.where(first_lane, 0.0, pltpu.roll(u, 1, 1))

    def after_z(u):
        return jnp.where(last_lane, 0.0, pltpu.roll(u, nz - 1, 1))

    def pair_sums(u):
        t = u.reshape(tiles)
        t = t + jnp.where(even_row, pltpu.roll(t, 7, 1), pltpu.roll(t, 1, 1))
        u = t.reshape(shape)
        return u + jnp.where(even_lane, pltpu.roll(u, nz - 1, 1), pltpu.roll(u, 1, 1))

    def forward(u):
        back = before_z(u)
        a, d = u + back, u - back
        ab, db = before_y(a), before_y(d)
        return a + ab, a - ab, d + db, d - db

    def inverse(t):
        t00, t10, t01, t11 = t
        ts = (t00 + t10) + after_y(t00 - t10)
        td = (t01 + t11) + after_y(t01 - t11)
        return (ts + td) + after_z(ts - td)

    def element(low, high, i):
        e1, e2, e3 = scales[0, i], scales[1, i], scales[2, i]
        m00 = e1 * (high[0] - low[0])
        s10, d10 = e1 * (high[1] + low[1]), e2 * (high[1] - low[1])
        s01, d01 = e1 * (high[2] + low[2]), e2 * (high[2] - low[2])
        s11, d11 = e2 * (high[3] + low[3]), e3 * (high[3] - low[3])
        return (m00, s10 + d10, s01 + d01, s11 + d11), (-m00, s10 - d10, s01 - d01, s11 - d11)

    def both(low, high, i):
        e1, e2 = scales[0, i], scales[1, i]
        return e1 * (high[1] + low[1]), e1 * (high[2] + low[2]), e2 * (high[3] + low[3])

    def plane_apply(value, start, stop):
        spectrum = once(lambda p: forward(value(p)))
        parts = once(lambda i: element(spectrum(i - 1), spectrum(i), i))
        for p in range(start, stop):
            t = [u + v for u, v in zip(parts(p)[0], parts(p + 1)[1])]
            yield p, inverse(t) + spring[p] * value(p)

    def cell_sums(spectrum, start, stop):
        parts = once(lambda i: element(spectrum(i - 1), spectrum(i), i))
        for cell in range(start, stop):
            p = 2 * cell
            up, down = parts(p)[0], parts(p + 2)[1]
            mid = [2.0 * u for u in both(spectrum(p), spectrum(p + 1), p + 1)]
            t = [up[0] + down[0]] + [up[k + 1] + mid[k] + down[k + 1] for k in range(3)]
            yield cell, inverse(t)

    def coarse_sums(value, start, stop):
        spectrum = once(lambda cell: forward(value(cell)))
        for cell, total in cell_sums(lambda p: spectrum(p // 2), start, stop):
            p = 2 * cell
            yield cell, pair_sums(total + (spring[p] + spring[p + 1]) * value(cell))

    lo, hi = 2 * HALO, planes - 2 * HALO
    near = range(HALO - 1, HALO + group + 1)
    for j in others:
        wait_slab(HALO + j // ngy, j % ngy)
    pl.when(has_below)(lambda: wait_side(0))
    pl.when(has_above)(lambda: wait_side(HALO + group))

    def inside(p):
        if p < lo:
            return jnp.where(has_below, jnp.float32(1.0), jnp.float32(0.0))
        if p >= hi:
            return jnp.where(has_above, jnp.float32(1.0), jnp.float32(0.0))
        return None

    def shared(amount, value, p):
        there = inside(p)
        return amount / value if there is None else there * (amount / (value + (1.0 - there)))

    def stiff(p):
        return ext[1, p // 2, p % 2].reshape(shape)

    diagonals = {}
    for p in range(lo - 3, hi + 4):
        e = stiff(p)
        scales[0, p] = e * (1.0 / 16.0)
        scales[1, p] = e * (1.0 / 24.0)
        scales[2, p] = e * (1.0 / 48.0)
        if p < hi + 3:
            tied = SPRING * ext[2, p // 2, p % 2].reshape(shape)
            spring[p] = tied
            around = e + stiff(p + 1)
            around = around + after_y(around)
            around = around + after_z(around)
            diagonals[p] = around * (1.0 / 3.0) + tied
            weight[p] = shared(OMEGA, diagonals[p], p)
        if p % 2 and p // 2 in near:
            cstep[p // 2] = shared(DAMP, pair_sums(diagonals[p - 1] + diagonals[p]), p)

    def swap_edges(low_src, high_src, low_dst, high_dst, k):
        down = pltpu.make_async_remote_copy(
            src_ref=low_src, dst_ref=high_dst, send_sem=x_send.at[k, 0], recv_sem=x_recv.at[k, 1],
            device_id=(jnp.maximum(gx - group, 0), gy), device_id_type=MESH)
        up = pltpu.make_async_remote_copy(
            src_ref=high_src, dst_ref=low_dst, send_sem=x_send.at[k, 1], recv_sem=x_recv.at[k, 0],
            device_id=(jnp.minimum(gx + group, ngx - 1), gy), device_id_type=MESH)
        pl.when(has_below)(down.start)
        pl.when(has_above)(up.start)
        return down, up

    def finish_edges(down, up):
        pl.when(has_below)(up.wait_recv)
        pl.when(has_above)(down.wait_recv)

    def drain_edges(down, up):
        pl.when(has_below)(down.wait_send)
        pl.when(has_above)(up.wait_send)

    pending = []

    def correct(source, call, meanwhile=lambda: None):
        def z(p):
            return source(p) * weight[p]

        spectrum = once(lambda p: forward(z(p)))
        for cell, total in cell_sums(spectrum, near.start, near.stop):
            p = 2 * cell
            given = (source(p) - spring[p] * z(p)) + (source(p + 1) - spring[p + 1] * z(p + 1))
            value = pair_sums(given - total)
            rest[cell] = value
            coarse[cell] = cstep[cell] * value
        for cell, total in coarse_sums(lambda c: coarse[c], HALO, HALO + group):
            own_c[call, cell - HALO] = coarse[cell] + cstep[cell] * (rest[cell] - total)
        copies = swap_edges(
            own_c.at[call, pl.ds(0, HALO)], own_c.at[call, pl.ds(group - HALO, HALO)],
            halo_c.at[call, 0], halo_c.at[call, 1], call)
        pending.append(copies)
        meanwhile()
        finish_edges(*copies)

        def swept(cell):
            if cell < HALO:
                return halo_c[call, 0, cell]
            if cell < HALO + group:
                return own_c[call, cell - HALO]
            return halo_c[call, 1, cell - HALO - group]

        for cell, total in coarse_sums(swept, near.start, near.stop):
            c = swept(cell) + cstep[cell] * (rest[cell] - total)
            for p in (2 * cell, 2 * cell + 1):
                smooth[p] = z(p) + c

    def smoothed(source, start, stop):
        for p, product in plane_apply(lambda p: smooth[p], start, stop):
            yield p, smooth[p] + weight[p] * (source(p) - product)

    def keep(f, p, u):
        fields[f, (p - lo) // 2, (p - lo) % 2] = u.reshape(ngy, ly, nz)

    def given_plane(p):
        return ext[0, p // 2, p % 2].reshape(shape)

    correct(given_plane, 0)
    for p, u in smoothed(given_plane, lo - 1, hi + 1):
        first[p] = u
        if lo <= p < hi:
            keep(0, p, u)
    for p, u in plane_apply(lambda p: first[p], lo, hi):
        keep(1, p, u)

    copies = swap_edges(
        fields.at[1, pl.ds(0, 2)], fields.at[1, pl.ds(group - 2, 2)], halo_a.at[0], halo_a.at[1], 2)
    pending.append(copies)

    def back_copy(k, f, n, j):
        return pltpu.make_async_remote_copy(
            src_ref=fields.at[pl.ds(f, n), j // ngy, :, j % ngy], dst_ref=returned.at[pl.ds(f, n), me],
            send_sem=b_send.at[k, j], recv_sem=b_recv.at[k, me],
            device_id=member(g, j), device_id_type=MESH)

    def wait_back(k, f, n, j):
        pltpu.make_async_remote_copy(
            src_ref=fields.at[pl.ds(f, n), 0, :, 0], dst_ref=returned.at[pl.ds(f, n), j],
            send_sem=b_send.at[k, j], recv_sem=b_recv.at[k, j],
            device_id=(gx, gy), device_id_type=MESH).wait_recv()

    def send_back(k, f, n):
        for j in others:
            back_copy(k, f, n, j).start()
        for i in range(f, f + n):
            returned[i, me] = fields[i, s, :, gy]

    send_back(0, 0, 2)
    finish_edges(*copies)

    def product_plane(p):
        if p < lo:
            u = halo_a[0, p // 2, p % 2]
        elif p < hi:
            u = fields[1, (p - lo) // 2, (p - lo) % 2]
        else:
            u = halo_a[1, (p - hi) // 2, (p - hi) % 2]
        return u.reshape(shape)

    def sum_copy(k, t):
        to = (t // ngy, t % ngy) if direct else member(g, t)
        return pltpu.make_async_remote_copy(
            src_ref=part.at[k], dst_ref=first_sums.at[k, seat], send_sem=a_send.at[k, t],
            recv_sem=a_recv.at[k, seat], device_id=to, device_id_type=MESH)

    def sum_wait(k, t):
        pltpu.make_async_remote_copy(
            src_ref=part.at[k], dst_ref=first_sums.at[k, t], send_sem=a_send.at[k, t],
            recv_sem=a_recv.at[k, t], device_id=(gx, gy), device_id_type=MESH).wait_recv()

    def total_copy(k, q):
        return pltpu.make_async_remote_copy(
            src_ref=group_sum.at[k], dst_ref=last_sums.at[k, g], send_sem=q_send.at[k, q],
            recv_sem=q_recv.at[k, g], device_id=(q * group + s, gy), device_id_type=MESH)

    def total_wait(k, q):
        pltpu.make_async_remote_copy(
            src_ref=group_sum.at[k], dst_ref=last_sums.at[k, q], send_sem=q_send.at[k, q],
            recv_sem=q_recv.at[k, q], device_id=(gx, gy), device_id_type=MESH).wait_recv()

    def start_sum(k, value):
        part[k] = jnp.zeros((count, 128), jnp.float32)
        part[k, :, 0 : value.shape[1]] = value
        for t in teammates:
            sum_copy(k, t).start()
        first_sums[k, seat] = part[k]

    def carry_sum(k):
        for t in teammates:
            sum_wait(k, t)
        group_sum[k] = jnp.sum(first_sums[k], axis=0)
        if direct:
            return
        for q in other_groups:
            total_copy(k, q).start()
        last_sums[k, g] = group_sum[k]

    def finish_sum(k):
        if direct:
            return group_sum[k]
        for q in other_groups:
            total_wait(k, q)
        return jnp.sum(last_sums[k], axis=0)

    def flat(block):
        parts = []
        for a in range(lx):
            turned = jnp.swapaxes(block[:, a], 0, 1)
            parts += [turned[b] for b in range(ly)]
        return jnp.concatenate(parts, axis=1)

    def dot(left, right, dims):
        return lax.dot_general(
            left, right, (dims, ((), ())), precision=EXACT, preferred_element_type=jnp.float32)

    def first_products():
        for j in others:
            wait_back(0, 0, 2, j)
        field, product, given = flat(returned[0]), flat(returned[1]), flat(pack[:, 0])
        flats[0], flats[1], flats[2] = field, product, given
        start_sum(0, dot(field, jnp.concatenate([product, given], axis=0), ((1,), (1,))))

    correct(product_plane, 1, first_products)
    carry_sum(0)
    for p, u in smoothed(product_plane, lo, hi):
        keep(2, p, u)
    send_back(1, 2, 1)

    field, product, given = flats[0], flats[1], flats[2]
    system = finish_sum(0)

    lane = axis_ids(system.shape, 1)
    row = axis_ids(system.shape, 0)
    crossed = jnp.transpose(system[:, 0:count])
    square = 0.5 * (system[:, 0:count] + crossed)
    same = axis_ids((count, count), 0) == axis_ids((count, count), 1)
    unit = jnp.where(same, 1.0, 0.0)
    rest_of = jnp.zeros((count, 128 - 4 * count), jnp.float32)
    system = jnp.concatenate([square, system[:, count : 2 * count], crossed, unit, rest_of], axis=1)
    for k in range(count):
        column = jnp.sum(jnp.where(lane == k, system, 0.0), axis=1, keepdims=True)
        pivot_row = system[k : k + 1]
        scaled = pivot_row / pivot_row[:, k : k + 1]
        system = jnp.where(row == k, scaled, system - column * scaled)

    def columns(n):
        return system[:, n * count : (n + 1) * count]

    step, turned_field, inverse_square = columns(1), columns(2), columns(3)

    def mixed(coef, u):
        return dot(coef, u, ((0,), (0,)))

    stores = []

    def put(n, target, u):
        for a in range(lx):
            at = a * ly
            block = jnp.stack([u[:, (at + b) * nz : (at + b + 1) * nz] for b in range(ly)], axis=0)
            outs[n, :, a] = jnp.swapaxes(block, 0, 1)
        stores.append(pltpu.make_async_copy(outs.at[n], target, out_sem.at[n]))
        stores[-1].start()

    put(0, sol_hbm, mixed(step, field))
    put(1, res_hbm, given - mixed(step, product))

    for j in others:
        wait_back(1, 2, 1, j)
    twice = flat(returned[2])
    start_sum(1, dot(product, twice, ((1,), (1,))))
    base = field - mixed(step, twice)
    carry_sum(1)
    second = finish_sum(1)[:, 0:count]

    def times(a, b):
        return jnp.dot(a, b, precision=EXACT, preferred_element_type=jnp.float32)

    turn = times(inverse_square, times(second, step)) - turned_field
    put(2, dir_hbm, base + mixed(turn, field))

    outward(lambda copy: copy.wait_send())
    for j in others:
        gather_copy(0, j).wait_send()
    for copies in pending:
        drain_edges(*copies)
    for k, f, n in ((0, 0, 2), (1, 2, 1)):
        for j in others:
            back_copy(k, f, n, j).wait_send()
    for k in range(2):
        for t in teammates:
            sum_copy(k, t).wait_send()
        if not direct:
            for q in other_groups:
                total_copy(k, q).wait_send()
    for store in stores:
        store.wait()


def hand_over(sol_in, res_in, dir_in, sol_out, res_out, dir_out, sems):
    pairs = ((sol_in, sol_out), (res_in, res_out), (dir_in, dir_out))
    copies = [pltpu.make_async_copy(source, target, sems.at[n]) for n, (source, target) in enumerate(pairs)]
    for copy in copies:
        copy.start()
    for copy in copies:
        copy.wait()


def local(ngx, ngy, rhs, classes, supports):
    count, lx, ly, nz = rhs.shape
    group = count // ngy
    groups = ngx // group
    slots = group + 2 * HALO
    rows = ngy * ly
    planes = 2 * slots
    team = ngx * ngy if ngx * ngy <= DIRECT else count
    f32 = jnp.float32
    dma = pltpu.SemaphoreType.DMA
    results = pl.pallas_call(
        functools.partial(kernel, ngx, ngy),
        out_shape=[jax.ShapeDtypeStruct(rhs.shape, f32)] * 3,
        in_specs=[pl.BlockSpec(memory_space=pltpu.HBM)] * 3,
        out_specs=[pl.BlockSpec(memory_space=pltpu.HBM)] * 3,
        scratch_shapes=[
            pltpu.VMEM(classes.shape, jnp.int32),
            pltpu.VMEM(supports.shape, jnp.int32),
            pltpu.VMEM((3, count, lx, ly, nz), f32),
            pltpu.VMEM((3, count, lx * ly * nz), f32),
            pltpu.VMEM((count, 3, lx, ly, nz), f32),
            pltpu.VMEM((3, slots, 2, ngy, ly, nz), f32),
            pltpu.VMEM((3, planes, rows, nz), f32),
            pltpu.VMEM((planes, rows, nz), f32),
            pltpu.VMEM((planes, rows, nz), f32),
            pltpu.VMEM((slots, rows, nz), f32),
            pltpu.VMEM((slots, rows, nz), f32),
            pltpu.VMEM((slots, rows, nz), f32),
            pltpu.VMEM((planes, rows, nz), f32),
            pltpu.VMEM((planes, rows, nz), f32),
            pltpu.VMEM((2, group, rows, nz), f32),
            pltpu.VMEM((2, 2, HALO, rows, nz), f32),
            pltpu.VMEM((2, 2, 2, ngy, ly, nz), f32),
            pltpu.VMEM((3, group, 2, ngy, ly, nz), f32),
            pltpu.VMEM((3, count, lx, ly, nz), f32),
            pltpu.VMEM((2, count, 128), f32),
            pltpu.VMEM((2, team, count, 128), f32),
            pltpu.VMEM((2, count, 128), f32),
            pltpu.VMEM((2, groups, count, 128), f32),
            dma((3,)), dma((3,)), dma((3, count)), dma((slots, ngy)),
            dma((3, 2)), dma((3, 2)), dma((2, count)), dma((2, count)),
            dma((2, team)), dma((2, team)), dma((2, groups)), dma((2, groups)),
        ],
        compiler_params=pltpu.CompilerParams(
            collective_id=0, has_side_effects=True),
        name="block_step",
    )(rhs, classes, supports)
    return pl.pallas_call(
        hand_over,
        out_shape=[jax.ShapeDtypeStruct(rhs.shape, f32)] * 3,
        in_specs=[pl.BlockSpec(memory_space=pltpu.HBM)] * 3,
        out_specs=[pl.BlockSpec(memory_space=pltpu.HBM)] * 3,
        scratch_shapes=[dma((3,))],
        name="hand_over",
    )(*results)


def solution(mesh):
    ngx, ngy = mesh.shape["gx"], mesh.shape["gy"]
    spread_out = P(None, "gx", "gy", None)
    return jax.shard_map(
        functools.partial(local, ngx, ngy),
        mesh=mesh,
        in_specs=(spread_out, P("gx", "gy", None), P("gx", "gy", None)),
        out_specs=(spread_out, spread_out, spread_out),
        check_vma=False,
    )
```

```python
import functools

import jax
import jax.numpy as jnp
from jax import lax
from jax.experimental import pallas as pl
from jax.experimental.pallas import tpu as pltpu
from jax.sharding import PartitionSpec as P

SPRING = 8.0
OMEGA = 0.6
DAMP = 0.5
HALO = 2

DIRECT = 0

MESH = pl.DeviceIdType.MESH
EXACT = lax.Precision.HIGHEST


def axis_ids(shape, dim):
    return lax.broadcasted_iota(jnp.int32, shape, dim)


def once(f):
    return functools.cache(f)


def kernel(
    ngx, ngy,
    rhs_ref, coef_ref, sol_ref, res_ref, dir_ref,
    flats, pack, ext, scales, weight, spring, cstep, rest, coarse, smooth, first,
    own_c, halo_c, halo_a, fields, returned, part, first_sums, group_sum, last_sums,
    g_send, g_recv, x_send, x_recv, b_send, b_recv, a_send, a_recv, q_send, q_recv,
):
    count, lx, ly, nz = rhs_ref.shape
    group = count // ngy
    groups = ngx // group
    slots = group + 2 * HALO
    rows = ngy * ly
    planes = 2 * slots
    gx, gy = lax.axis_index("gx"), lax.axis_index("gy")
    g, s = gx // group, gx % group
    me = s * ngy + gy

    def each(size, at, action):
        @pl.loop(1, size)
        def _(o):
            action((at + o) % size)

    others = functools.partial(each, count, me)
    other_groups = functools.partial(each, groups, g)

    devices = ngx * ngy
    direct = devices <= DIRECT
    place = gx * ngy + gy
    team, seat = (devices, place) if direct else (count, me)
    teammates = functools.partial(each, team, seat)

    def member(at_group, j):
        return (at_group * group + j // ngy, j % ngy)

    barrier = pltpu.get_barrier_semaphore()

    def greet(target):
        pl.semaphore_signal(barrier, inc=1, device_id=target, device_id_type=MESH)

    def greet_group(at_group):
        @pl.loop(0, count)
        def _(j):
            greet(member(at_group, j))

    has_below, has_above = g > 0, g < groups - 1
    if direct:
        teammates(lambda t: greet((t // ngy, t % ngy)))
        expected = devices - 1
    else:
        others(lambda j: greet(member(g, j)))
        pl.when(has_below)(lambda: greet_group(g - 1))
        pl.when(has_above)(lambda: greet_group(g + 1))
        for q in range(groups):
            pl.when(jnp.abs(q - g) > 1)(functools.partial(greet, (q * group + s, gy)))
        below, above = has_below.astype(jnp.int32), has_above.astype(jnp.int32)
        expected = (count - 1) + count * (below + above) + (groups - 1 - below - above)

    def clear(side):
        at = 0 if side == 0 else slots - HALO
        ext[:, at : at + HALO] = jnp.zeros((3, HALO, 2, ngy, ly, nz), jnp.float32)
        for call in range(2):
            halo_c[call, side] = jnp.zeros((HALO, rows, nz), jnp.float32)
        halo_a[side] = jnp.zeros((2, 2, ngy, ly, nz), jnp.float32)

    pl.when(g == 0)(lambda: clear(0))
    pl.when(g == groups - 1)(lambda: clear(1))
    pack[:, 0] = rhs_ref[...]
    for j in range(count):
        pack[j, 1:3] = coef_ref[...]
    pl.semaphore_wait(barrier, expected)

    def gather_copy(dg, j):
        slot = s + HALO - dg * group
        return pltpu.make_async_remote_copy(
            src_ref=pack.at[j], dst_ref=ext.at[:, slot, :, gy],
            send_sem=g_send.at[dg + 1, j], recv_sem=g_recv.at[slot, gy],
            device_id=member(g + dg, j), device_id_type=MESH)

    def outward(action):
        for dg, there in ((-1, has_below), (1, has_above)):
            slot = s + HALO - dg * group

            @pl.when(there & (slot >= 0) & (slot < slots))
            def _():
                @pl.loop(0, count)
                def _(j):
                    action(gather_copy(dg, j))

    outward(lambda copy: copy.start())
    others(lambda j: gather_copy(0, j).start())
    ext[:, s + HALO, :, gy] = pack[me]

    def wait_slab(slot, y):
        pltpu.make_async_remote_copy(
            src_ref=pack.at[0], dst_ref=ext.at[:, slot, :, y], send_sem=g_send.at[0, 0],
            recv_sem=g_recv.at[slot, y], device_id=(gx, gy), device_id_type=MESH).wait_recv()

    def wait_side(at):
        @pl.loop(0, HALO * ngy)
        def _(i):
            wait_slab(at + i // ngy, i % ngy)

    shape = (rows, nz)
    row_id, lane_id = axis_ids(shape, 0), axis_ids(shape, 1)
    first_row, last_row = row_id == 0, row_id == rows - 1
    first_lane, last_lane = lane_id == 0, lane_id == nz - 1
    tiles = (rows // 8, 8, nz)
    even_row, even_lane = axis_ids(tiles, 1) % 2 == 0, lane_id % 2 == 0

    def before_y(u):
        return jnp.where(first_row, 0.0, pltpu.roll(u, 1, 0))

    def after_y(u):
        return jnp.where(last_row, 0.0, pltpu.roll(u, rows - 1, 0))

    def before_z(u):
        return jnp.where(first_lane, 0.0, pltpu.roll(u, 1, 1))

    def after_z(u):
        return jnp.where(last_lane, 0.0, pltpu.roll(u, nz - 1, 1))

    def pair_sums(u):
        t = u.reshape(tiles)
        t = t + jnp.where(even_row, pltpu.roll(t, 7, 1), pltpu.roll(t, 1, 1))
        u = t.reshape(shape)
        return u + jnp.where(even_lane, pltpu.roll(u, nz - 1, 1), pltpu.roll(u, 1, 1))

    def forward(u):
        back = before_z(u)
        a, d = u + back, u - back
        ab, db = before_y(a), before_y(d)
        return a + ab, a - ab, d + db, d - db

    def inverse(t):
        t00, t10, t01, t11 = t
        ts = (t00 + t10) + after_y(t00 - t10)
        td = (t01 + t11) + after_y(t01 - t11)
        return (ts + td) + after_z(ts - td)

    def element(low, high, i):
        e1, e2, e3 = scales[0, i], scales[1, i], scales[2, i]
        m00 = e1 * (high[0] - low[0])
        s10, d10 = e1 * (high[1] + low[1]), e2 * (high[1] - low[1])
        s01, d01 = e1 * (high[2] + low[2]), e2 * (high[2] - low[2])
        s11, d11 = e2 * (high[3] + low[3]), e3 * (high[3] - low[3])
        return (m00, s10 + d10, s01 + d01, s11 + d11), (-m00, s10 - d10, s01 - d01, s11 - d11)

    def both(low, high, i):
        e1, e2 = scales[0, i], scales[1, i]
        return e1 * (high[1] + low[1]), e1 * (high[2] + low[2]), e2 * (high[3] + low[3])

    def plane_apply(value, start, stop):
        spectrum = once(lambda p: forward(value(p)))
        parts = once(lambda i: element(spectrum(i - 1), spectrum(i), i))
        for p in range(start, stop):
            t = [u + v for u, v in zip(parts(p)[0], parts(p + 1)[1])]
            yield p, inverse(t) + spring[p] * value(p)

    def cell_sums(spectrum, start, stop):
        parts = once(lambda i: element(spectrum(i - 1), spectrum(i), i))
        for cell in range(start, stop):
            p = 2 * cell
            up, down = parts(p)[0], parts(p + 2)[1]
            mid = [2.0 * u for u in both(spectrum(p), spectrum(p + 1), p + 1)]
            t = [up[0] + down[0]] + [up[k + 1] + mid[k] + down[k + 1] for k in range(3)]
            yield cell, inverse(t)

    def coarse_sums(value, start, stop):
        spectrum = once(lambda cell: forward(value(cell)))
        for cell, total in cell_sums(lambda p: spectrum(p // 2), start, stop):
            p = 2 * cell
            yield cell, pair_sums(total + (spring[p] + spring[p + 1]) * value(cell))

    lo, hi = 2 * HALO, planes - 2 * HALO
    near = range(HALO - 1, HALO + group + 1)
    others(lambda j: wait_slab(HALO + j // ngy, j % ngy))
    pl.when(has_below)(lambda: wait_side(0))
    pl.when(has_above)(lambda: wait_side(HALO + group))

    def inside(p):
        if p < lo:
            return jnp.where(has_below, jnp.float32(1.0), jnp.float32(0.0))
        if p >= hi:
            return jnp.where(has_above, jnp.float32(1.0), jnp.float32(0.0))
        return None

    def shared(amount, value, p):
        there = inside(p)
        return amount / value if there is None else there * (amount / (value + (1.0 - there)))

    def stiff(p):
        return ext[1, p // 2, p % 2].reshape(shape)

    diagonals = {}
    for p in range(lo - 3, hi + 4):
        e = stiff(p)
        scales[0, p] = e * (1.0 / 16.0)
        scales[1, p] = e * (1.0 / 24.0)
        scales[2, p] = e * (1.0 / 48.0)
        if p < hi + 3:
            tied = SPRING * ext[2, p // 2, p % 2].reshape(shape)
            spring[p] = tied
            around = e + stiff(p + 1)
            around = around + after_y(around)
            around = around + after_z(around)
            diagonals[p] = around * (1.0 / 3.0) + tied
            weight[p] = shared(OMEGA, diagonals[p], p)
        if p % 2 and p // 2 in near:
            cstep[p // 2] = shared(DAMP, pair_sums(diagonals[p - 1] + diagonals[p]), p)

    def swap_edges(low_src, high_src, low_dst, high_dst, k):
        down = pltpu.make_async_remote_copy(
            src_ref=low_src, dst_ref=high_dst, send_sem=x_send.at[k, 0], recv_sem=x_recv.at[k, 1],
            device_id=(jnp.maximum(gx - group, 0), gy), device_id_type=MESH)
        up = pltpu.make_async_remote_copy(
            src_ref=high_src, dst_ref=low_dst, send_sem=x_send.at[k, 1], recv_sem=x_recv.at[k, 0],
            device_id=(jnp.minimum(gx + group, ngx - 1), gy), device_id_type=MESH)
        pl.when(has_below)(down.start)
        pl.when(has_above)(up.start)
        return down, up

    def finish_edges(down, up):
        pl.when(has_below)(up.wait_recv)
        pl.when(has_above)(down.wait_recv)

    def drain_edges(down, up):
        pl.when(has_below)(down.wait_send)
        pl.when(has_above)(up.wait_send)

    pending = []

    def correct(source, call, meanwhile=lambda: None):
        def z(p):
            return source(p) * weight[p]

        spectrum = once(lambda p: forward(z(p)))
        for cell, total in cell_sums(spectrum, near.start, near.stop):
            p = 2 * cell
            given = (source(p) - spring[p] * z(p)) + (source(p + 1) - spring[p + 1] * z(p + 1))
            value = pair_sums(given - total)
            rest[cell] = value
            coarse[cell] = cstep[cell] * value
        for cell, total in coarse_sums(lambda c: coarse[c], HALO, HALO + group):
            own_c[call, cell - HALO] = coarse[cell] + cstep[cell] * (rest[cell] - total)
        copies = swap_edges(
            own_c.at[call, pl.ds(0, HALO)], own_c.at[call, pl.ds(group - HALO, HALO)],
            halo_c.at[call, 0], halo_c.at[call, 1], call)
        pending.append(copies)
        meanwhile()
        finish_edges(*copies)

        def swept(cell):
            if cell < HALO:
                return halo_c[call, 0, cell]
            if cell < HALO + group:
                return own_c[call, cell - HALO]
            return halo_c[call, 1, cell - HALO - group]

        for cell, total in coarse_sums(swept, near.start, near.stop):
            c = swept(cell) + cstep[cell] * (rest[cell] - total)
            for p in (2 * cell, 2 * cell + 1):
                smooth[p] = z(p) + c

    def smoothed(source, start, stop):
        for p, product in plane_apply(lambda p: smooth[p], start, stop):
            yield p, smooth[p] + weight[p] * (source(p) - product)

    def keep(f, p, u):
        fields[f, (p - lo) // 2, (p - lo) % 2] = u.reshape(ngy, ly, nz)

    def given_plane(p):
        return ext[0, p // 2, p % 2].reshape(shape)

    correct(given_plane, 0)
    for p, u in smoothed(given_plane, lo - 1, hi + 1):
        first[p] = u
        if lo <= p < hi:
            keep(0, p, u)
    for p, u in plane_apply(lambda p: first[p], lo, hi):
        keep(1, p, u)

    copies = swap_edges(
        fields.at[1, pl.ds(0, 2)], fields.at[1, pl.ds(group - 2, 2)], halo_a.at[0], halo_a.at[1], 2)
    pending.append(copies)

    def back_copy(k, f, n, j):
        return pltpu.make_async_remote_copy(
            src_ref=fields.at[pl.ds(f, n), j // ngy, :, j % ngy], dst_ref=returned.at[pl.ds(f, n), me],
            send_sem=b_send.at[k, j], recv_sem=b_recv.at[k, me],
            device_id=member(g, j), device_id_type=MESH)

    def wait_back(k, f, n, j):
        pltpu.make_async_remote_copy(
            src_ref=fields.at[pl.ds(f, n), 0, :, 0], dst_ref=returned.at[pl.ds(f, n), j],
            send_sem=b_send.at[k, j], recv_sem=b_recv.at[k, j],
            device_id=(gx, gy), device_id_type=MESH).wait_recv()

    def send_back(k, f, n):
        others(lambda j: back_copy(k, f, n, j).start())
        for i in range(f, f + n):
            returned[i, me] = fields[i, s, :, gy]

    send_back(0, 0, 2)
    finish_edges(*copies)

    def product_plane(p):
        if p < lo:
            u = halo_a[0, p // 2, p % 2]
        elif p < hi:
            u = fields[1, (p - lo) // 2, (p - lo) % 2]
        else:
            u = halo_a[1, (p - hi) // 2, (p - hi) % 2]
        return u.reshape(shape)

    def sum_copy(k, t):
        to = (t // ngy, t % ngy) if direct else member(g, t)
        return pltpu.make_async_remote_copy(
            src_ref=part.at[k], dst_ref=first_sums.at[k, seat], send_sem=a_send.at[k, t],
            recv_sem=a_recv.at[k, seat], device_id=to, device_id_type=MESH)

    def sum_wait(k, t):
        pltpu.make_async_remote_copy(
            src_ref=part.at[k], dst_ref=first_sums.at[k, t], send_sem=a_send.at[k, t],
            recv_sem=a_recv.at[k, t], device_id=(gx, gy), device_id_type=MESH).wait_recv()

    def total_copy(k, q):
        return pltpu.make_async_remote_copy(
            src_ref=group_sum.at[k], dst_ref=last_sums.at[k, g], send_sem=q_send.at[k, q],
            recv_sem=q_recv.at[k, g], device_id=(q * group + s, gy), device_id_type=MESH)

    def total_wait(k, q):
        pltpu.make_async_remote_copy(
            src_ref=group_sum.at[k], dst_ref=last_sums.at[k, q], send_sem=q_send.at[k, q],
            recv_sem=q_recv.at[k, q], device_id=(gx, gy), device_id_type=MESH).wait_recv()

    def start_sum(k, value):
        part[k] = jnp.zeros((count, 128), jnp.float32)
        part[k, :, 0 : value.shape[1]] = value
        teammates(lambda t: sum_copy(k, t).start())
        first_sums[k, seat] = part[k]

    def carry_sum(k):
        teammates(lambda t: sum_wait(k, t))
        group_sum[k] = jnp.sum(first_sums[k], axis=0)
        if direct:
            return
        other_groups(lambda q: total_copy(k, q).start())
        last_sums[k, g] = group_sum[k]

    def finish_sum(k):
        if direct:
            return group_sum[k]
        other_groups(lambda q: total_wait(k, q))
        return jnp.sum(last_sums[k], axis=0)

    def flat(block):
        parts = []
        for a in range(lx):
            turned = jnp.swapaxes(block[:, a], 0, 1)
            parts += [turned[b] for b in range(ly)]
        return jnp.concatenate(parts, axis=1)

    def dot(left, right, dims):
        return lax.dot_general(
            left, right, (dims, ((), ())), precision=EXACT, preferred_element_type=jnp.float32)

    def first_products():
        others(lambda j: wait_back(0, 0, 2, j))
        field, product, given = flat(returned[0]), flat(returned[1]), flat(pack[:, 0])
        flats[0], flats[1], flats[2] = field, product, given
        start_sum(0, dot(field, jnp.concatenate([product, given], axis=0), ((1,), (1,))))

    correct(product_plane, 1, first_products)
    carry_sum(0)
    for p, u in smoothed(product_plane, lo, hi):
        keep(2, p, u)
    send_back(1, 2, 1)

    field, product, given = flats[0], flats[1], flats[2]
    system = finish_sum(0)

    lane = axis_ids(system.shape, 1)
    row = axis_ids(system.shape, 0)
    crossed = jnp.transpose(system[:, 0:count])
    square = 0.5 * (system[:, 0:count] + crossed)
    same = axis_ids((count, count), 0) == axis_ids((count, count), 1)
    unit = jnp.where(same, 1.0, 0.0)
    rest_of = jnp.zeros((count, 128 - 4 * count), jnp.float32)
    system = jnp.concatenate([square, system[:, count : 2 * count], crossed, unit, rest_of], axis=1)
    for k in range(count):
        column = jnp.sum(jnp.where(lane == k, system, 0.0), axis=1, keepdims=True)
        pivot_row = system[k : k + 1]
        scaled = pivot_row / pivot_row[:, k : k + 1]
        system = jnp.where(row == k, scaled, system - column * scaled)

    def columns(n):
        return system[:, n * count : (n + 1) * count]

    step, turned_field, inverse_square = columns(1), columns(2), columns(3)

    def mixed(coef, u):
        return dot(coef, u, ((0,), (0,)))

    def put(target, u):
        for a in range(lx):
            at = a * ly
            block = jnp.stack([u[:, (at + b) * nz : (at + b + 1) * nz] for b in range(ly)], axis=0)
            target[:, a] = jnp.swapaxes(block, 0, 1)

    put(sol_ref, mixed(step, field))
    put(res_ref, given - mixed(step, product))

    others(lambda j: wait_back(1, 2, 1, j))
    twice = flat(returned[2])
    start_sum(1, dot(product, twice, ((1,), (1,))))
    base = field - mixed(step, twice)
    carry_sum(1)
    second = finish_sum(1)[:, 0:count]

    def times(a, b):
        return jnp.dot(a, b, precision=EXACT, preferred_element_type=jnp.float32)

    turn = times(inverse_square, times(second, step)) - turned_field
    put(dir_ref, base + mixed(turn, field))

    outward(lambda copy: copy.wait_send())
    others(lambda j: gather_copy(0, j).wait_send())
    for copies in pending:
        drain_edges(*copies)
    for k, f, n in ((0, 0, 2), (1, 2, 1)):
        others(lambda j: back_copy(k, f, n, j).wait_send())
    for k in range(2):
        teammates(lambda t: sum_copy(k, t).wait_send())
        if not direct:
            other_groups(lambda q: total_copy(k, q).wait_send())


def hand_over(sol_in, res_in, dir_in, sol_out, res_out, dir_out, sems):
    pairs = ((sol_in, sol_out), (res_in, res_out), (dir_in, dir_out))
    copies = [pltpu.make_async_copy(source, target, sems.at[n]) for n, (source, target) in enumerate(pairs)]
    for copy in copies:
        copy.start()
    for copy in copies:
        copy.wait()


def local(ngx, ngy, rhs, classes, supports):
    count, lx, ly, nz = rhs.shape
    group = count // ngy
    groups = ngx // group
    slots = group + 2 * HALO
    rows = ngy * ly
    planes = 2 * slots
    team = ngx * ngy if ngx * ngy <= DIRECT else count
    f32 = jnp.float32
    dma = pltpu.SemaphoreType.DMA
    density = (classes.astype(f32) + 1.0) / 4.0
    coef = jnp.stack([0.001 + density * density * density, supports.astype(f32)])
    results = pl.pallas_call(
        functools.partial(kernel, ngx, ngy),
        out_shape=[jax.ShapeDtypeStruct(rhs.shape, f32)] * 3,
        in_specs=[pl.BlockSpec(memory_space=pltpu.VMEM)] * 2,
        out_specs=[pl.BlockSpec(memory_space=pltpu.VMEM)] * 3,
        scratch_shapes=[
            pltpu.VMEM((3, count, lx * ly * nz), f32),
            pltpu.VMEM((count, 3, lx, ly, nz), f32),
            pltpu.VMEM((3, slots, 2, ngy, ly, nz), f32),
            pltpu.VMEM((3, planes, rows, nz), f32),
            pltpu.VMEM((planes, rows, nz), f32),
            pltpu.VMEM((planes, rows, nz), f32),
            pltpu.VMEM((slots, rows, nz), f32),
            pltpu.VMEM((slots, rows, nz), f32),
            pltpu.VMEM((slots, rows, nz), f32),
            pltpu.VMEM((planes, rows, nz), f32),
            pltpu.VMEM((planes, rows, nz), f32),
            pltpu.VMEM((2, group, rows, nz), f32),
            pltpu.VMEM((2, 2, HALO, rows, nz), f32),
            pltpu.VMEM((2, 2, 2, ngy, ly, nz), f32),
            pltpu.VMEM((3, group, 2, ngy, ly, nz), f32),
            pltpu.VMEM((3, count, lx, ly, nz), f32),
            pltpu.VMEM((2, count, 128), f32),
            pltpu.VMEM((2, team, count, 128), f32),
            pltpu.VMEM((2, count, 128), f32),
            pltpu.VMEM((2, groups, count, 128), f32),
            dma((3, count)), dma((slots, ngy)),
            dma((3, 2)), dma((3, 2)), dma((2, count)), dma((2, count)),
            dma((2, team)), dma((2, team)), dma((2, groups)), dma((2, groups)),
        ],
        compiler_params=pltpu.CompilerParams(
            collective_id=0, has_side_effects=True, vmem_limit_bytes=32 * 1024 * 1024),
        name="block_step",
    )(rhs, coef)
    return pl.pallas_call(
        hand_over,
        out_shape=[jax.ShapeDtypeStruct(rhs.shape, f32)] * 3,
        in_specs=[pl.BlockSpec(memory_space=pltpu.VMEM)] * 3,
        out_specs=[pl.BlockSpec(memory_space=pltpu.HBM)] * 3,
        compiler_params=pltpu.CompilerParams(vmem_limit_bytes=4 * 1024 * 1024),
        scratch_shapes=[dma((3,))],
        name="hand_over",
    )(*results)


def solution(mesh):
    ngx, ngy = mesh.shape["gx"], mesh.shape["gy"]
    spread_out = P(None, "gx", "gy", None)
    return jax.shard_map(
        functools.partial(local, ngx, ngy),
        mesh=mesh,
        in_specs=(spread_out, P("gx", "gy", None), P("gx", "gy", None)),
        out_specs=(spread_out, spread_out, spread_out),
        check_vma=False,
    )
```

```python
import functools

import jax
import jax.numpy as jnp
from jax import lax
from jax.experimental import pallas as pl
from jax.experimental.pallas import tpu as pltpu
from jax.sharding import PartitionSpec as P

SPRING = 8.0
OMEGA = 0.6
DAMP = 0.5
HALO = 2

MESH = pl.DeviceIdType.MESH
EXACT = lax.Precision.HIGHEST


def axis_ids(shape, dim):
    return lax.broadcasted_iota(jnp.int32, shape, dim)


def once(f):
    return functools.cache(f)


def halves(u):
    top = u.astype(jnp.bfloat16)
    return top, (u - top.astype(jnp.float32)).astype(jnp.bfloat16)


def kernel(
    ngx, ngy,
    rhs_ref, mine, sol_ref, res_ref, dir_ref,
    cext, rext, scales, weight, spring, cstep, rest, coarse, smooth, first,
    own_c, halo_c, halo_a, fields, returned, part, first_sums, group_sum, last_sums,
    gc_send, gc_recv, gr_send, gr_recv, x_send, x_recv, b_send, b_recv, a_send, a_recv, q_send, q_recv,
):
    count, lx, ly, nz = rhs_ref.shape
    group = count // ngy
    groups = ngx // group
    slots = group + 2 * HALO
    rows = ngy * ly
    planes = 2 * slots
    gx, gy = lax.axis_index("gx"), lax.axis_index("gy")
    g, s = gx // group, gx % group
    me = s * ngy + gy
    others = [(me + o) % count for o in range(1, count)]
    other_groups = [(g + o) % groups for o in range(1, groups)]

    def member(at_group, j):
        return (at_group * group + j // ngy, j % ngy)

    barrier = pltpu.get_barrier_semaphore()

    def greet(target):
        pl.semaphore_signal(barrier, inc=1, device_id=target, device_id_type=MESH)

    def greet_group(at_group):
        for j in range(count):
            greet(member(at_group, j))

    has_below, has_above = g > 0, g < groups - 1
    for j in others:
        greet(member(g, j))
    pl.when(has_below)(lambda: greet_group(g - 1))
    pl.when(has_above)(lambda: greet_group(g + 1))
    for q in range(groups):
        pl.when(jnp.abs(q - g) > 1)(functools.partial(greet, (q * group + s, gy)))
    below, above = has_below.astype(jnp.int32), has_above.astype(jnp.int32)
    expected = (count - 1) + count * (below + above) + (groups - 1 - below - above)

    def clear(side):
        at = 0 if side == 0 else slots - HALO
        cext[:, at : at + HALO] = jnp.zeros((2, HALO, 2, ngy, ly, nz), jnp.float32)
        rext[at : at + HALO] = jnp.zeros((HALO, 2, ngy, ly, nz), jnp.float32)
        for call in range(2):
            halo_c[call, side] = jnp.zeros((HALO, rows, nz), jnp.float32)
        halo_a[side] = jnp.zeros((2, 2, ngy, ly, nz), jnp.float32)

    pl.when(g == 0)(lambda: clear(0))
    pl.when(g == groups - 1)(lambda: clear(1))
    pl.semaphore_wait(barrier, expected)

    def coef_copy(dg, j):
        slot = s + HALO - dg * group
        return pltpu.make_async_remote_copy(
            src_ref=mine, dst_ref=cext.at[:, slot, :, gy],
            send_sem=gc_send.at[dg + 1, j], recv_sem=gc_recv.at[slot, gy],
            device_id=member(g + dg, j), device_id_type=MESH)

    def rhs_copy(dg, j):
        slot = s + HALO - dg * group
        return pltpu.make_async_remote_copy(
            src_ref=rhs_ref.at[j], dst_ref=rext.at[slot, :, gy],
            send_sem=gr_send.at[dg + 1, j], recv_sem=gr_recv.at[slot, gy],
            device_id=member(g + dg, j), device_id_type=MESH)

    def outward(action):
        for dg, there in ((-1, has_below), (1, has_above)):
            slot = s + HALO - dg * group

            @pl.when(there & (slot >= 0) & (slot < slots))
            def _():
                for make in (coef_copy, rhs_copy):
                    for j in range(count):
                        action(make(dg, j))

    outward(lambda copy: copy.start())
    for make in (coef_copy, rhs_copy):
        for j in others:
            make(0, j).start()
    cext[:, s + HALO, :, gy] = mine[...]
    rext[s + HALO, :, gy] = rhs_ref[me]

    def wait_coef(slot, y):
        pltpu.make_async_remote_copy(
            src_ref=mine, dst_ref=cext.at[:, slot, :, y], send_sem=gc_send.at[0, 0],
            recv_sem=gc_recv.at[slot, y], device_id=(gx, gy), device_id_type=MESH).wait_recv()

    def wait_rhs(slot, y):
        pltpu.make_async_remote_copy(
            src_ref=rhs_ref.at[0], dst_ref=rext.at[slot, :, y], send_sem=gr_send.at[0, 0],
            recv_sem=gr_recv.at[slot, y], device_id=(gx, gy), device_id_type=MESH).wait_recv()

    def wait_all(wait):
        def side(at):
            for slot in range(at, at + HALO):
                for y in range(ngy):
                    wait(slot, y)

        for j in others:
            wait(HALO + j // ngy, j % ngy)
        pl.when(has_below)(lambda: side(0))
        pl.when(has_above)(lambda: side(HALO + group))

    shape = (rows, nz)
    row_id, lane_id = axis_ids(shape, 0), axis_ids(shape, 1)
    first_row, last_row = row_id == 0, row_id == rows - 1
    first_lane, last_lane = lane_id == 0, lane_id == nz - 1
    tiles = (rows // 8, 8, nz)
    even_row, even_lane = axis_ids(tiles, 1) % 2 == 0, lane_id % 2 == 0

    def before_y(u):
        return jnp.where(first_row, 0.0, pltpu.roll(u, 1, 0))

    def after_y(u):
        return jnp.where(last_row, 0.0, pltpu.roll(u, rows - 1, 0))

    def before_z(u):
        return jnp.where(first_lane, 0.0, pltpu.roll(u, 1, 1))

    def after_z(u):
        return jnp.where(last_lane, 0.0, pltpu.roll(u, nz - 1, 1))

    def pair_sums(u):
        t = u.reshape(tiles)
        t = t + jnp.where(even_row, pltpu.roll(t, 7, 1), pltpu.roll(t, 1, 1))
        u = t.reshape(shape)
        return u + jnp.where(even_lane, pltpu.roll(u, nz - 1, 1), pltpu.roll(u, 1, 1))

    def forward(u):
        back = before_z(u)
        a, d = u + back, u - back
        ab, db = before_y(a), before_y(d)
        return a + ab, a - ab, d + db, d - db

    def inverse(t):
        t00, t10, t01, t11 = t
        ts = (t00 + t10) + after_y(t00 - t10)
        td = (t01 + t11) + after_y(t01 - t11)
        return (ts + td) + after_z(ts - td)

    def element(low, high, i):
        e1, e2, e3 = scales[0, i], scales[1, i], scales[2, i]
        m00 = e1 * (high[0] - low[0])
        s10, d10 = e1 * (high[1] + low[1]), e2 * (high[1] - low[1])
        s01, d01 = e1 * (high[2] + low[2]), e2 * (high[2] - low[2])
        s11, d11 = e2 * (high[3] + low[3]), e3 * (high[3] - low[3])
        return (m00, s10 + d10, s01 + d01, s11 + d11), (-m00, s10 - d10, s01 - d01, s11 - d11)

    def both(low, high, i):
        e1, e2 = scales[0, i], scales[1, i]
        return e1 * (high[1] + low[1]), e1 * (high[2] + low[2]), e2 * (high[3] + low[3])

    def plane_apply(value, start, stop):
        spectrum = once(lambda p: forward(value(p)))
        parts = once(lambda i: element(spectrum(i - 1), spectrum(i), i))
        for p in range(start, stop):
            t = [u + v for u, v in zip(parts(p)[0], parts(p + 1)[1])]
            yield p, inverse(t) + spring[p] * value(p)

    def cell_sums(spectrum, start, stop):
        parts = once(lambda i: element(spectrum(i - 1), spectrum(i), i))
        for cell in range(start, stop):
            p = 2 * cell
            up, down = parts(p)[0], parts(p + 2)[1]
            mid = [2.0 * u for u in both(spectrum(p), spectrum(p + 1), p + 1)]
            t = [up[0] + down[0]] + [up[k + 1] + mid[k] + down[k + 1] for k in range(3)]
            yield cell, inverse(t)

    def coarse_sums(value, start, stop):
        spectrum = once(lambda cell: forward(value(cell)))
        for cell, total in cell_sums(lambda p: spectrum(p // 2), start, stop):
            p = 2 * cell
            yield cell, pair_sums(total + (spring[p] + spring[p + 1]) * value(cell))

    lo, hi = 2 * HALO, planes - 2 * HALO
    near = range(HALO - 1, HALO + group + 1)
    wait_all(wait_coef)

    def inside(p):
        if p < lo:
            return jnp.where(has_below, jnp.float32(1.0), jnp.float32(0.0))
        if p >= hi:
            return jnp.where(has_above, jnp.float32(1.0), jnp.float32(0.0))
        return None

    def shared(amount, value, p):
        there = inside(p)
        return amount / value if there is None else there * (amount / (value + (1.0 - there)))

    def stiff(p):
        return cext[0, p // 2, p % 2].reshape(shape)

    diagonals = {}
    for p in range(lo - 3, hi + 4):
        e = stiff(p)
        scales[0, p] = e * (1.0 / 16.0)
        scales[1, p] = e * (1.0 / 24.0)
        scales[2, p] = e * (1.0 / 48.0)
        if p < hi + 3:
            tied = SPRING * cext[1, p // 2, p % 2].reshape(shape)
            spring[p] = tied
            around = e + stiff(p + 1)
            around = around + after_y(around)
            around = around + after_z(around)
            diagonals[p] = around * (1.0 / 3.0) + tied
            weight[p] = shared(OMEGA, diagonals[p], p)
        if p % 2 and p // 2 in near:
            cstep[p // 2] = shared(DAMP, pair_sums(diagonals[p - 1] + diagonals[p]), p)

    def swap_edges(low_src, high_src, low_dst, high_dst, k):
        down = pltpu.make_async_remote_copy(
            src_ref=low_src, dst_ref=high_dst, send_sem=x_send.at[k, 0], recv_sem=x_recv.at[k, 1],
            device_id=(jnp.maximum(gx - group, 0), gy), device_id_type=MESH)
        up = pltpu.make_async_remote_copy(
            src_ref=high_src, dst_ref=low_dst, send_sem=x_send.at[k, 1], recv_sem=x_recv.at[k, 0],
            device_id=(jnp.minimum(gx + group, ngx - 1), gy), device_id_type=MESH)
        pl.when(has_below)(down.start)
        pl.when(has_above)(up.start)
        return down, up

    def finish_edges(down, up):
        pl.when(has_below)(up.wait_recv)
        pl.when(has_above)(down.wait_recv)

    def drain_edges(down, up):
        pl.when(has_below)(down.wait_send)
        pl.when(has_above)(up.wait_send)

    pending = []

    def correct(source, call):
        def z(p):
            return source(p) * weight[p]

        spectrum = once(lambda p: forward(z(p)))
        for cell, total in cell_sums(spectrum, near.start, near.stop):
            p = 2 * cell
            given = (source(p) - spring[p] * z(p)) + (source(p + 1) - spring[p + 1] * z(p + 1))
            value = pair_sums(given - total)
            rest[cell] = value
            coarse[cell] = cstep[cell] * value
        for cell, total in coarse_sums(lambda c: coarse[c], HALO, HALO + group):
            own_c[call, cell - HALO] = coarse[cell] + cstep[cell] * (rest[cell] - total)
        copies = swap_edges(
            own_c.at[call, pl.ds(0, HALO)], own_c.at[call, pl.ds(group - HALO, HALO)],
            halo_c.at[call, 0], halo_c.at[call, 1], call)
        pending.append(copies)
        finish_edges(*copies)

        def swept(cell):
            if cell < HALO:
                return halo_c[call, 0, cell]
            if cell < HALO + group:
                return own_c[call, cell - HALO]
            return halo_c[call, 1, cell - HALO - group]

        for cell, total in coarse_sums(swept, near.start, near.stop):
            c = swept(cell) + cstep[cell] * (rest[cell] - total)
            for p in (2 * cell, 2 * cell + 1):
                smooth[p] = z(p) + c

    def smoothed(source, start, stop):
        for p, product in plane_apply(lambda p: smooth[p], start, stop):
            yield p, smooth[p] + weight[p] * (source(p) - product)

    def keep(f, p, u):
        fields[f, (p - lo) // 2, (p - lo) % 2] = u.reshape(ngy, ly, nz)

    wait_all(wait_rhs)

    def given_plane(p):
        return rext[p // 2, p % 2].reshape(shape)

    correct(given_plane, 0)
    for p, u in smoothed(given_plane, lo - 1, hi + 1):
        first[p] = u
        if lo <= p < hi:
            keep(0, p, u)
    for p, u in plane_apply(lambda p: first[p], lo, hi):
        keep(1, p, u)

    copies = swap_edges(
        fields.at[1, pl.ds(0, 2)], fields.at[1, pl.ds(group - 2, 2)], halo_a.at[0], halo_a.at[1], 2)
    pending.append(copies)

    def back_copy(k, f, n, j):
        return pltpu.make_async_remote_copy(
            src_ref=fields.at[pl.ds(f, n), j // ngy, :, j % ngy], dst_ref=returned.at[pl.ds(f, n), me],
            send_sem=b_send.at[k, j], recv_sem=b_recv.at[k, me],
            device_id=member(g, j), device_id_type=MESH)

    def wait_back(k, f, n, j):
        pltpu.make_async_remote_copy(
            src_ref=fields.at[pl.ds(f, n), 0, :, 0], dst_ref=returned.at[pl.ds(f, n), j],
            send_sem=b_send.at[k, j], recv_sem=b_recv.at[k, j],
            device_id=(gx, gy), device_id_type=MESH).wait_recv()

    def send_back(k, f, n):
        for j in others:
            back_copy(k, f, n, j).start()
        for i in range(f, f + n):
            returned[i, me] = fields[i, s, :, gy]

    send_back(0, 0, 2)
    finish_edges(*copies)

    def product_plane(p):
        if p < lo:
            u = halo_a[0, p // 2, p % 2]
        elif p < hi:
            u = fields[1, (p - lo) // 2, (p - lo) % 2]
        else:
            u = halo_a[1, (p - hi) // 2, (p - hi) % 2]
        return u.reshape(shape)

    correct(product_plane, 1)
    for p, u in smoothed(product_plane, lo, hi):
        keep(2, p, u)
    send_back(1, 2, 1)

    def flat(block):
        parts = []
        for a in range(lx):
            turned = jnp.swapaxes(block[:, a], 0, 1)
            parts += [turned[b] for b in range(ly)]
        return jnp.concatenate(parts, axis=1)

    given = flat(rhs_ref[...])
    for j in others:
        wait_back(0, 0, 2, j)
    field, product = flat(returned[0]), flat(returned[1])
    for j in others:
        wait_back(1, 2, 1, j)
    twice = flat(returned[2])

    def dot(left, right, dims):
        return lax.dot_general(left, right, (dims, ((), ())), preferred_element_type=jnp.float32)

    left_top, left_low = halves(jnp.concatenate([field, product], axis=0))
    right_top, right_low = halves(jnp.concatenate([product, given, field, twice], axis=0))
    sums = dot(
        jnp.concatenate([left_top, left_low, left_top], axis=1),
        jnp.concatenate([right_top, right_top, right_low], axis=1), ((1,), (1,)))
    wide = 4 * count
    lane = axis_ids((count, wide), 1)
    part[...] = jnp.zeros_like(part)
    part[:, 0:wide] = jnp.where(lane < 2 * count, sums[:count], sums[count:])

    def sum_copy(j):
        return pltpu.make_async_remote_copy(
            src_ref=part, dst_ref=first_sums.at[me], send_sem=a_send.at[j], recv_sem=a_recv.at[me],
            device_id=member(g, j), device_id_type=MESH)

    def sum_wait(j):
        pltpu.make_async_remote_copy(
            src_ref=part, dst_ref=first_sums.at[j], send_sem=a_send.at[j], recv_sem=a_recv.at[j],
            device_id=(gx, gy), device_id_type=MESH).wait_recv()

    for j in others:
        sum_copy(j).start()
    first_sums[me] = part[...]
    for j in others:
        sum_wait(j)
    group_sum[...] = jnp.sum(first_sums[...], axis=0)

    def total_copy(q):
        return pltpu.make_async_remote_copy(
            src_ref=group_sum, dst_ref=last_sums.at[g], send_sem=q_send.at[q], recv_sem=q_recv.at[g],
            device_id=(q * group + s, gy), device_id_type=MESH)

    def total_wait(q):
        pltpu.make_async_remote_copy(
            src_ref=group_sum, dst_ref=last_sums.at[q], send_sem=q_send.at[q], recv_sem=q_recv.at[q],
            device_id=(gx, gy), device_id_type=MESH).wait_recv()

    for q in other_groups:
        total_copy(q).start()
    last_sums[g] = group_sum[...]
    for q in other_groups:
        total_wait(q)
    system = jnp.sum(last_sums[...], axis=0)

    lane = axis_ids(system.shape, 1)
    row = axis_ids(system.shape, 0)
    mirrored = pltpu.roll(system, system.shape[1] - 2 * count, 1)
    system = jnp.where(lane < count, 0.5 * (system + mirrored), system)
    for k in range(count):
        column = jnp.sum(jnp.where(lane == k, system, 0.0), axis=1, keepdims=True)
        pivot_row = system[k : k + 1]
        scaled = pivot_row / pivot_row[:, k : k + 1]
        system = jnp.where(row == k, scaled, system - column * scaled)

    def columns(n):
        return system[:, n * count : (n + 1) * count]

    step = columns(1)
    turn = jnp.dot(columns(3), step, precision=EXACT, preferred_element_type=jnp.float32) - columns(2)

    def mixed(coef, u):
        coef_top, u_top = [v.astype(jnp.bfloat16).astype(jnp.float32) for v in (coef, u)]
        coefs = jnp.concatenate([coef_top, coef - coef_top, coef_top], axis=0).astype(jnp.bfloat16)
        terms = jnp.concatenate([u_top, u_top, u - u_top], axis=0).astype(jnp.bfloat16)
        return dot(coefs, terms, ((0,), (0,)))

    def put(ref, u):
        for a in range(lx):
            at = a * ly
            block = jnp.stack([u[:, (at + b) * nz : (at + b + 1) * nz] for b in range(ly)], axis=0)
            ref[:, a] = jnp.swapaxes(block, 0, 1)

    put(sol_ref, mixed(step, field))
    put(res_ref, given - mixed(step, product))
    put(dir_ref, field + mixed(jnp.concatenate([turn, -step], axis=0), jnp.concatenate([field, twice], axis=0)))

    outward(lambda copy: copy.wait_send())
    for make in (coef_copy, rhs_copy):
        for j in others:
            make(0, j).wait_send()
    for copies in pending:
        drain_edges(*copies)
    for k, f, n in ((0, 0, 2), (1, 2, 1)):
        for j in others:
            back_copy(k, f, n, j).wait_send()
    for j in others:
        sum_copy(j).wait_send()
    for q in other_groups:
        total_copy(q).wait_send()


def hand_over(sol_in, res_in, dir_in, sol_out, res_out, dir_out, sems):
    pairs = ((sol_in, sol_out), (res_in, res_out), (dir_in, dir_out))
    copies = [pltpu.make_async_copy(source, target, sems.at[n]) for n, (source, target) in enumerate(pairs)]
    for copy in copies:
        copy.start()
    for copy in copies:
        copy.wait()


def local(ngx, ngy, rhs, classes, supports):
    count, lx, ly, nz = rhs.shape
    group = count // ngy
    groups = ngx // group
    slots = group + 2 * HALO
    rows = ngy * ly
    planes = 2 * slots
    f32 = jnp.float32
    dma = pltpu.SemaphoreType.DMA
    density = (classes.astype(f32) + 1.0) / 4.0
    coef = jnp.stack([0.001 + density * density * density, supports.astype(f32)])
    results = pl.pallas_call(
        functools.partial(kernel, ngx, ngy),
        out_shape=[jax.ShapeDtypeStruct(rhs.shape, f32)] * 3,
        in_specs=[pl.BlockSpec(memory_space=pltpu.VMEM)] * 2,
        out_specs=[pl.BlockSpec(memory_space=pltpu.VMEM)] * 3,
        scratch_shapes=[
            pltpu.VMEM((2, slots, 2, ngy, ly, nz), f32),
            pltpu.VMEM((slots, 2, ngy, ly, nz), f32),
            pltpu.VMEM((3, planes, rows, nz), f32),
            pltpu.VMEM((planes, rows, nz), f32),
            pltpu.VMEM((planes, rows, nz), f32),
            pltpu.VMEM((slots, rows, nz), f32),
            pltpu.VMEM((slots, rows, nz), f32),
            pltpu.VMEM((slots, rows, nz), f32),
            pltpu.VMEM((planes, rows, nz), f32),
            pltpu.VMEM((planes, rows, nz), f32),
            pltpu.VMEM((2, group, rows, nz), f32),
            pltpu.VMEM((2, 2, HALO, rows, nz), f32),
            pltpu.VMEM((2, 2, 2, ngy, ly, nz), f32),
            pltpu.VMEM((3, group, 2, ngy, ly, nz), f32),
            pltpu.VMEM((3, count, lx, ly, nz), f32),
            pltpu.VMEM((count, 128), f32),
            pltpu.VMEM((count, count, 128), f32),
            pltpu.VMEM((count, 128), f32),
            pltpu.VMEM((groups, count, 128), f32),
            dma((3, count)), dma((slots, ngy)), dma((3, count)), dma((slots, ngy)),
            dma((3, 2)), dma((3, 2)), dma((2, count)), dma((2, count)),
            dma((count,)), dma((count,)), dma((groups,)), dma((groups,)),
        ],
        compiler_params=pltpu.CompilerParams(
            collective_id=0, has_side_effects=True, vmem_limit_bytes=32 * 1024 * 1024),
        name="block_step",
    )(rhs, coef)
    return pl.pallas_call(
        hand_over,
        out_shape=[jax.ShapeDtypeStruct(rhs.shape, f32)] * 3,
        in_specs=[pl.BlockSpec(memory_space=pltpu.VMEM)] * 3,
        out_specs=[pl.BlockSpec(memory_space=pltpu.HBM)] * 3,
        compiler_params=pltpu.CompilerParams(vmem_limit_bytes=4 * 1024 * 1024),
        scratch_shapes=[dma((3,))],
        name="hand_over",
    )(*results)


def solution(mesh):
    ngx, ngy = mesh.shape["gx"], mesh.shape["gy"]
    spread_out = P(None, "gx", "gy", None)
    return jax.shard_map(
        functools.partial(local, ngx, ngy),
        mesh=mesh,
        in_specs=(spread_out, P("gx", "gy", None), P("gx", "gy", None)),
        out_specs=(spread_out, spread_out, spread_out),
        check_vma=False,
    )
```

```python
import functools

import jax
import jax.numpy as jnp
from jax import lax
from jax.experimental import pallas as pl
from jax.experimental.pallas import tpu as pltpu
from jax.sharding import PartitionSpec as P

SPRING = 8.0
OMEGA = 0.6
DAMP = 0.5
HALO = 2

MESH = pl.DeviceIdType.MESH
EXACT = lax.Precision.HIGHEST


def axis_ids(shape, dim):
    return lax.broadcasted_iota(jnp.int32, shape, dim)


def once(f):
    return functools.cache(f)


def halves(u):
    top = u.astype(jnp.bfloat16)
    return top, (u - top.astype(jnp.float32)).astype(jnp.bfloat16)


def kernel(
    ngx, ngy,
    rhs_ref, mine, sol_ref, res_ref, dir_ref,
    cext, rext, scales, weight, spring, cstep, rest, coarse, smooth, first,
    own_c, halo_c, halo_a, fields, returned, part, first_sums, group_sum, last_sums,
    gc_send, gc_recv, gr_send, gr_recv, x_send, x_recv, b_send, b_recv, a_send, a_recv, q_send, q_recv,
):
    count, lx, ly, nz = rhs_ref.shape
    group = count // ngy
    groups = ngx // group
    slots = group + 2 * HALO
    rows = ngy * ly
    planes = 2 * slots
    gx, gy = lax.axis_index("gx"), lax.axis_index("gy")
    g, s = gx // group, gx % group
    me = s * ngy + gy
    others = [(me + o) % count for o in range(1, count)]
    other_groups = [(g + o) % groups for o in range(1, groups)]

    def member(at_group, j):
        return (at_group * group + j // ngy, j % ngy)

    barrier = pltpu.get_barrier_semaphore()

    def greet(target):
        pl.semaphore_signal(barrier, inc=1, device_id=target, device_id_type=MESH)

    def greet_group(at_group):
        for j in range(count):
            greet(member(at_group, j))

    has_below, has_above = g > 0, g < groups - 1
    for j in others:
        greet(member(g, j))
    pl.when(has_below)(lambda: greet_group(g - 1))
    pl.when(has_above)(lambda: greet_group(g + 1))
    for q in range(groups):
        pl.when(jnp.abs(q - g) > 1)(functools.partial(greet, (q * group + s, gy)))
    below, above = has_below.astype(jnp.int32), has_above.astype(jnp.int32)
    expected = (count - 1) + count * (below + above) + (groups - 1 - below - above)

    def clear(side):
        at = 0 if side == 0 else slots - HALO
        cext[:, at : at + HALO] = jnp.zeros((2, HALO, 2, ngy, ly, nz), jnp.float32)
        rext[at : at + HALO] = jnp.zeros((HALO, 2, ngy, ly, nz), jnp.float32)
        for call in range(2):
            halo_c[call, side] = jnp.zeros((HALO, rows, nz), jnp.float32)
        halo_a[side] = jnp.zeros((2, 2, ngy, ly, nz), jnp.float32)

    pl.when(g == 0)(lambda: clear(0))
    pl.when(g == groups - 1)(lambda: clear(1))
    pl.semaphore_wait(barrier, expected)

    def coef_copy(dg, j):
        slot = s + HALO - dg * group
        return pltpu.make_async_remote_copy(
            src_ref=mine, dst_ref=cext.at[:, slot, :, gy],
            send_sem=gc_send.at[dg + 1, j], recv_sem=gc_recv.at[slot, gy],
            device_id=member(g + dg, j), device_id_type=MESH)

    def rhs_copy(dg, j):
        slot = s + HALO - dg * group
        return pltpu.make_async_remote_copy(
            src_ref=rhs_ref.at[j], dst_ref=rext.at[slot, :, gy],
            send_sem=gr_send.at[dg + 1, j], recv_sem=gr_recv.at[slot, gy],
            device_id=member(g + dg, j), device_id_type=MESH)

    def outward(action):
        for dg, there in ((-1, has_below), (1, has_above)):
            slot = s + HALO - dg * group

            @pl.when(there & (slot >= 0) & (slot < slots))
            def _():
                for make in (coef_copy, rhs_copy):
                    for j in range(count):
                        action(make(dg, j))

    outward(lambda copy: copy.start())
    for make in (coef_copy, rhs_copy):
        for j in others:
            make(0, j).start()
    cext[:, s + HALO, :, gy] = mine[...]
    rext[s + HALO, :, gy] = rhs_ref[me]

    def wait_coef(slot, y):
        pltpu.make_async_remote_copy(
            src_ref=mine, dst_ref=cext.at[:, slot, :, y], send_sem=gc_send.at[0, 0],
            recv_sem=gc_recv.at[slot, y], device_id=(gx, gy), device_id_type=MESH).wait_recv()

    def wait_rhs(slot, y):
        pltpu.make_async_remote_copy(
            src_ref=rhs_ref.at[0], dst_ref=rext.at[slot, :, y], send_sem=gr_send.at[0, 0],
            recv_sem=gr_recv.at[slot, y], device_id=(gx, gy), device_id_type=MESH).wait_recv()

    def wait_all(wait):
        def side(at):
            for slot in range(at, at + HALO):
                for y in range(ngy):
                    wait(slot, y)

        for j in others:
            wait(HALO + j // ngy, j % ngy)
        pl.when(has_below)(lambda: side(0))
        pl.when(has_above)(lambda: side(HALO + group))

    shape = (rows, nz)
    row_id, lane_id = axis_ids(shape, 0), axis_ids(shape, 1)
    first_row, last_row = row_id == 0, row_id == rows - 1
    first_lane, last_lane = lane_id == 0, lane_id == nz - 1
    tiles = (rows // 8, 8, nz)
    even_row, even_lane = axis_ids(tiles, 1) % 2 == 0, lane_id % 2 == 0

    def before_y(u):
        return jnp.where(first_row, 0.0, pltpu.roll(u, 1, 0))

    def after_y(u):
        return jnp.where(last_row, 0.0, pltpu.roll(u, rows - 1, 0))

    def before_z(u):
        return jnp.where(first_lane, 0.0, pltpu.roll(u, 1, 1))

    def after_z(u):
        return jnp.where(last_lane, 0.0, pltpu.roll(u, nz - 1, 1))

    def pair_sums(u):
        t = u.reshape(tiles)
        t = t + jnp.where(even_row, pltpu.roll(t, 7, 1), pltpu.roll(t, 1, 1))
        u = t.reshape(shape)
        return u + jnp.where(even_lane, pltpu.roll(u, nz - 1, 1), pltpu.roll(u, 1, 1))

    def forward(u):
        back = before_z(u)
        a, d = u + back, u - back
        ab, db = before_y(a), before_y(d)
        return a + ab, a - ab, d + db, d - db

    def inverse(t):
        t00, t10, t01, t11 = t
        ts = (t00 + t10) + after_y(t00 - t10)
        td = (t01 + t11) + after_y(t01 - t11)
        return (ts + td) + after_z(ts - td)

    def element(low, high, i):
        e1, e2, e3 = scales[0, i], scales[1, i], scales[2, i]
        m00 = e1 * (high[0] - low[0])
        s10, d10 = e1 * (high[1] + low[1]), e2 * (high[1] - low[1])
        s01, d01 = e1 * (high[2] + low[2]), e2 * (high[2] - low[2])
        s11, d11 = e2 * (high[3] + low[3]), e3 * (high[3] - low[3])
        return (m00, s10 + d10, s01 + d01, s11 + d11), (-m00, s10 - d10, s01 - d01, s11 - d11)

    def both(low, high, i):
        e1, e2 = scales[0, i], scales[1, i]
        return e1 * (high[1] + low[1]), e1 * (high[2] + low[2]), e2 * (high[3] + low[3])

    def plane_apply(value, start, stop):
        spectrum = once(lambda p: forward(value(p)))
        parts = once(lambda i: element(spectrum(i - 1), spectrum(i), i))
        for p in range(start, stop):
            t = [u + v for u, v in zip(parts(p)[0], parts(p + 1)[1])]
            yield p, inverse(t) + spring[p] * value(p)

    def cell_sums(spectrum, start, stop):
        parts = once(lambda i: element(spectrum(i - 1), spectrum(i), i))
        for cell in range(start, stop):
            p = 2 * cell
            up, down = parts(p)[0], parts(p + 2)[1]
            mid = [2.0 * u for u in both(spectrum(p), spectrum(p + 1), p + 1)]
            t = [up[0] + down[0]] + [up[k + 1] + mid[k] + down[k + 1] for k in range(3)]
            yield cell, inverse(t)

    def coarse_sums(value, start, stop):
        spectrum = once(lambda cell: forward(value(cell)))
        for cell, total in cell_sums(lambda p: spectrum(p // 2), start, stop):
            p = 2 * cell
            yield cell, pair_sums(total + (spring[p] + spring[p + 1]) * value(cell))

    lo, hi = 2 * HALO, planes - 2 * HALO
    near = range(HALO - 1, HALO + group + 1)
    wait_all(wait_coef)

    def inside(p):
        if p < lo:
            return jnp.where(has_below, jnp.float32(1.0), jnp.float32(0.0))
        if p >= hi:
            return jnp.where(has_above, jnp.float32(1.0), jnp.float32(0.0))
        return None

    def shared(amount, value, p):
        there = inside(p)
        return amount / value if there is None else there * (amount / (value + (1.0 - there)))

    def stiff(p):
        return cext[0, p // 2, p % 2].reshape(shape)

    diagonals = {}
    for p in range(lo - 3, hi + 4):
        e = stiff(p)
        scales[0, p] = e * (1.0 / 16.0)
        scales[1, p] = e * (1.0 / 24.0)
        scales[2, p] = e * (1.0 / 48.0)
        if p < hi + 3:
            tied = SPRING * cext[1, p // 2, p % 2].reshape(shape)
            spring[p] = tied
            around = e + stiff(p + 1)
            around = around + after_y(around)
            around = around + after_z(around)
            diagonals[p] = around * (1.0 / 3.0) + tied
            weight[p] = shared(OMEGA, diagonals[p], p)
        if p % 2 and p // 2 in near:
            cstep[p // 2] = shared(DAMP, pair_sums(diagonals[p - 1] + diagonals[p]), p)

    def swap_edges(low_src, high_src, low_dst, high_dst, k):
        down = pltpu.make_async_remote_copy(
            src_ref=low_src, dst_ref=high_dst, send_sem=x_send.at[k, 0], recv_sem=x_recv.at[k, 1],
            device_id=(jnp.maximum(gx - group, 0), gy), device_id_type=MESH)
        up = pltpu.make_async_remote_copy(
            src_ref=high_src, dst_ref=low_dst, send_sem=x_send.at[k, 1], recv_sem=x_recv.at[k, 0],
            device_id=(jnp.minimum(gx + group, ngx - 1), gy), device_id_type=MESH)
        pl.when(has_below)(down.start)
        pl.when(has_above)(up.start)
        return down, up

    def finish_edges(down, up):
        pl.when(has_below)(up.wait_recv)
        pl.when(has_above)(down.wait_recv)

    def drain_edges(down, up):
        pl.when(has_below)(down.wait_send)
        pl.when(has_above)(up.wait_send)

    pending = []

    def correct(source, call, meanwhile=lambda: None):
        def z(p):
            return source(p) * weight[p]

        spectrum = once(lambda p: forward(z(p)))
        for cell, total in cell_sums(spectrum, near.start, near.stop):
            p = 2 * cell
            given = (source(p) - spring[p] * z(p)) + (source(p + 1) - spring[p + 1] * z(p + 1))
            value = pair_sums(given - total)
            rest[cell] = value
            coarse[cell] = cstep[cell] * value
        for cell, total in coarse_sums(lambda c: coarse[c], HALO, HALO + group):
            own_c[call, cell - HALO] = coarse[cell] + cstep[cell] * (rest[cell] - total)
        copies = swap_edges(
            own_c.at[call, pl.ds(0, HALO)], own_c.at[call, pl.ds(group - HALO, HALO)],
            halo_c.at[call, 0], halo_c.at[call, 1], call)
        pending.append(copies)
        meanwhile()
        finish_edges(*copies)

        def swept(cell):
            if cell < HALO:
                return halo_c[call, 0, cell]
            if cell < HALO + group:
                return own_c[call, cell - HALO]
            return halo_c[call, 1, cell - HALO - group]

        for cell, total in coarse_sums(swept, near.start, near.stop):
            c = swept(cell) + cstep[cell] * (rest[cell] - total)
            for p in (2 * cell, 2 * cell + 1):
                smooth[p] = z(p) + c

    def smoothed(source, start, stop):
        for p, product in plane_apply(lambda p: smooth[p], start, stop):
            yield p, smooth[p] + weight[p] * (source(p) - product)

    def keep(f, p, u):
        fields[f, (p - lo) // 2, (p - lo) % 2] = u.reshape(ngy, ly, nz)

    wait_all(wait_rhs)

    def given_plane(p):
        return rext[p // 2, p % 2].reshape(shape)

    correct(given_plane, 0)
    for p, u in smoothed(given_plane, lo - 1, hi + 1):
        first[p] = u
        if lo <= p < hi:
            keep(0, p, u)
    for p, u in plane_apply(lambda p: first[p], lo, hi):
        keep(1, p, u)

    copies = swap_edges(
        fields.at[1, pl.ds(0, 2)], fields.at[1, pl.ds(group - 2, 2)], halo_a.at[0], halo_a.at[1], 2)
    pending.append(copies)

    def back_copy(k, f, n, j):
        return pltpu.make_async_remote_copy(
            src_ref=fields.at[pl.ds(f, n), j // ngy, :, j % ngy], dst_ref=returned.at[pl.ds(f, n), me],
            send_sem=b_send.at[k, j], recv_sem=b_recv.at[k, me],
            device_id=member(g, j), device_id_type=MESH)

    def wait_back(k, f, n, j):
        pltpu.make_async_remote_copy(
            src_ref=fields.at[pl.ds(f, n), 0, :, 0], dst_ref=returned.at[pl.ds(f, n), j],
            send_sem=b_send.at[k, j], recv_sem=b_recv.at[k, j],
            device_id=(gx, gy), device_id_type=MESH).wait_recv()

    def send_back(k, f, n):
        for j in others:
            back_copy(k, f, n, j).start()
        for i in range(f, f + n):
            returned[i, me] = fields[i, s, :, gy]

    send_back(0, 0, 2)
    finish_edges(*copies)

    def product_plane(p):
        if p < lo:
            u = halo_a[0, p // 2, p % 2]
        elif p < hi:
            u = fields[1, (p - lo) // 2, (p - lo) % 2]
        else:
            u = halo_a[1, (p - hi) // 2, (p - hi) % 2]
        return u.reshape(shape)

    def flat(block):
        parts = []
        for a in range(lx):
            turned = jnp.swapaxes(block[:, a], 0, 1)
            parts += [turned[b] for b in range(ly)]
        return jnp.concatenate(parts, axis=1)

    flats = []

    def flatten():
        flats.append(flat(rhs_ref[...]))
        for j in others:
            wait_back(0, 0, 2, j)
        flats.extend((flat(returned[0]), flat(returned[1])))

    correct(product_plane, 1, flatten)
    given, field, product = flats
    for p, u in smoothed(product_plane, lo, hi):
        keep(2, p, u)
    send_back(1, 2, 1)

    for j in others:
        wait_back(1, 2, 1, j)
    twice = flat(returned[2])

    def dot(left, right, dims):
        return lax.dot_general(left, right, (dims, ((), ())), preferred_element_type=jnp.float32)

    left_top, left_low = halves(jnp.concatenate([field, product], axis=0))
    right_top, right_low = halves(jnp.concatenate([product, given, field, twice], axis=0))
    sums = dot(
        jnp.concatenate([left_top, left_low, left_top], axis=1),
        jnp.concatenate([right_top, right_top, right_low], axis=1), ((1,), (1,)))
    wide = 4 * count
    lane = axis_ids((count, wide), 1)
    part[...] = jnp.zeros_like(part)
    part[:, 0:wide] = jnp.where(lane < 2 * count, sums[:count], sums[count:])

    def sum_copy(j):
        return pltpu.make_async_remote_copy(
            src_ref=part, dst_ref=first_sums.at[me], send_sem=a_send.at[j], recv_sem=a_recv.at[me],
            device_id=member(g, j), device_id_type=MESH)

    def sum_wait(j):
        pltpu.make_async_remote_copy(
            src_ref=part, dst_ref=first_sums.at[j], send_sem=a_send.at[j], recv_sem=a_recv.at[j],
            device_id=(gx, gy), device_id_type=MESH).wait_recv()

    for j in others:
        sum_copy(j).start()
    first_sums[me] = part[...]
    for j in others:
        sum_wait(j)
    group_sum[...] = jnp.sum(first_sums[...], axis=0)

    def total_copy(q):
        return pltpu.make_async_remote_copy(
            src_ref=group_sum, dst_ref=last_sums.at[g], send_sem=q_send.at[q], recv_sem=q_recv.at[g],
            device_id=(q * group + s, gy), device_id_type=MESH)

    def total_wait(q):
        pltpu.make_async_remote_copy(
            src_ref=group_sum, dst_ref=last_sums.at[q], send_sem=q_send.at[q], recv_sem=q_recv.at[q],
            device_id=(gx, gy), device_id_type=MESH).wait_recv()

    for q in other_groups:
        total_copy(q).start()
    last_sums[g] = group_sum[...]
    for q in other_groups:
        total_wait(q)
    system = jnp.sum(last_sums[...], axis=0)

    lane = axis_ids(system.shape, 1)
    row = axis_ids(system.shape, 0)
    mirrored = pltpu.roll(system, system.shape[1] - 2 * count, 1)
    system = jnp.where(lane < count, 0.5 * (system + mirrored), system)
    for k in range(count):
        column = jnp.sum(jnp.where(lane == k, system, 0.0), axis=1, keepdims=True)
        pivot_row = system[k : k + 1]
        scaled = pivot_row / pivot_row[:, k : k + 1]
        system = jnp.where(row == k, scaled, system - column * scaled)

    def columns(n):
        return system[:, n * count : (n + 1) * count]

    step = columns(1)
    turn = jnp.dot(columns(3), step, precision=EXACT, preferred_element_type=jnp.float32) - columns(2)

    def mixed(coef, u):
        coef_top, u_top = [v.astype(jnp.bfloat16).astype(jnp.float32) for v in (coef, u)]
        coefs = jnp.concatenate([coef_top, coef - coef_top, coef_top], axis=0).astype(jnp.bfloat16)
        terms = jnp.concatenate([u_top, u_top, u - u_top], axis=0).astype(jnp.bfloat16)
        return dot(coefs, terms, ((0,), (0,)))

    def put(ref, u):
        for a in range(lx):
            at = a * ly
            block = jnp.stack([u[:, (at + b) * nz : (at + b + 1) * nz] for b in range(ly)], axis=0)
            ref[:, a] = jnp.swapaxes(block, 0, 1)

    put(sol_ref, mixed(step, field))
    put(res_ref, given - mixed(step, product))
    put(dir_ref, field + mixed(jnp.concatenate([turn, -step], axis=0), jnp.concatenate([field, twice], axis=0)))

    outward(lambda copy: copy.wait_send())
    for make in (coef_copy, rhs_copy):
        for j in others:
            make(0, j).wait_send()
    for copies in pending:
        drain_edges(*copies)
    for k, f, n in ((0, 0, 2), (1, 2, 1)):
        for j in others:
            back_copy(k, f, n, j).wait_send()
    for j in others:
        sum_copy(j).wait_send()
    for q in other_groups:
        total_copy(q).wait_send()


def hand_over(sol_in, res_in, dir_in, sol_out, res_out, dir_out, sems):
    pairs = ((sol_in, sol_out), (res_in, res_out), (dir_in, dir_out))
    copies = [pltpu.make_async_copy(source, target, sems.at[n]) for n, (source, target) in enumerate(pairs)]
    for copy in copies:
        copy.start()
    for copy in copies:
        copy.wait()


def local(ngx, ngy, rhs, classes, supports):
    count, lx, ly, nz = rhs.shape
    group = count // ngy
    groups = ngx // group
    slots = group + 2 * HALO
    rows = ngy * ly
    planes = 2 * slots
    f32 = jnp.float32
    dma = pltpu.SemaphoreType.DMA
    density = (classes.astype(f32) + 1.0) / 4.0
    coef = jnp.stack([0.001 + density * density * density, supports.astype(f32)])
    results = pl.pallas_call(
        functools.partial(kernel, ngx, ngy),
        out_shape=[jax.ShapeDtypeStruct(rhs.shape, f32)] * 3,
        in_specs=[pl.BlockSpec(memory_space=pltpu.VMEM)] * 2,
        out_specs=[pl.BlockSpec(memory_space=pltpu.VMEM)] * 3,
        scratch_shapes=[
            pltpu.VMEM((2, slots, 2, ngy, ly, nz), f32),
            pltpu.VMEM((slots, 2, ngy, ly, nz), f32),
            pltpu.VMEM((3, planes, rows, nz), f32),
            pltpu.VMEM((planes, rows, nz), f32),
            pltpu.VMEM((planes, rows, nz), f32),
            pltpu.VMEM((slots, rows, nz), f32),
            pltpu.VMEM((slots, rows, nz), f32),
            pltpu.VMEM((slots, rows, nz), f32),
            pltpu.VMEM((planes, rows, nz), f32),
            pltpu.VMEM((planes, rows, nz), f32),
            pltpu.VMEM((2, group, rows, nz), f32),
            pltpu.VMEM((2, 2, HALO, rows, nz), f32),
            pltpu.VMEM((2, 2, 2, ngy, ly, nz), f32),
            pltpu.VMEM((3, group, 2, ngy, ly, nz), f32),
            pltpu.VMEM((3, count, lx, ly, nz), f32),
            pltpu.VMEM((count, 128), f32),
            pltpu.VMEM((count, count, 128), f32),
            pltpu.VMEM((count, 128), f32),
            pltpu.VMEM((groups, count, 128), f32),
            dma((3, count)), dma((slots, ngy)), dma((3, count)), dma((slots, ngy)),
            dma((3, 2)), dma((3, 2)), dma((2, count)), dma((2, count)),
            dma((count,)), dma((count,)), dma((groups,)), dma((groups,)),
        ],
        compiler_params=pltpu.CompilerParams(
            collective_id=0, has_side_effects=True, vmem_limit_bytes=32 * 1024 * 1024),
        name="block_step",
    )(rhs, coef)
    return pl.pallas_call(
        hand_over,
        out_shape=[jax.ShapeDtypeStruct(rhs.shape, f32)] * 3,
        in_specs=[pl.BlockSpec(memory_space=pltpu.VMEM)] * 3,
        out_specs=[pl.BlockSpec(memory_space=pltpu.HBM)] * 3,
        compiler_params=pltpu.CompilerParams(vmem_limit_bytes=4 * 1024 * 1024),
        scratch_shapes=[dma((3,))],
        name="hand_over",
    )(*results)


def solution(mesh):
    ngx, ngy = mesh.shape["gx"], mesh.shape["gy"]
    spread_out = P(None, "gx", "gy", None)
    return jax.shard_map(
        functools.partial(local, ngx, ngy),
        mesh=mesh,
        in_specs=(spread_out, P("gx", "gy", None), P("gx", "gy", None)),
        out_specs=(spread_out, spread_out, spread_out),
        check_vma=False,
    )
```
